256 devices in a mesh: seq: 64 (over y, z, core), tp: 4 (over x).
Axes of the slice: x: 4, y: 4, z: 8, core: 2. Of those that a mesh axis runs over, the one named last changes fastest.
Arguments:
- signal: float32 [32, 1048576], P(None, ('seq', 'tp')), may hold values from -6 to 6
- filter_taps: float32 [32, 1048576], P(None, ('seq', 'tp')), as said below
- skip_gain: float32 [32], P('tp'), may hold values from -4 to 4
Outputs:
- output: float32 [32, 1048576], P('tp', 'seq')
The draws below stay inside these ranges and needn't reach their ends.
Inputs may be any that keep to these rules, and one draw needn't show every extreme that they name: `filter_taps`: filter taps are real values of both signs.
All inputs are finite; a program needn't handle non-finite values.
Results may differ from the reference program's by a relative error of at most 0.000082.
Values sent between devices are 32-bit elements; how exact they have to be, the bound alone decides.
No kernel may reach another device: no remote copies, remote signals or barrier semaphores. Data moves between devices by JAX's collectives and lax.ppermute only.
A program may use at most 64 MiB of HBM per device.

```python
import math
import jax
import jax.numpy as jnp

CHANNELS = 32
TOKENS = 1048576


def draw_filter_taps(key, part):
    rate_key, noise_key = jax.random.split(key, 2)
    rate = jnp.exp(jax.random.uniform(rate_key, (CHANNELS, 1), jnp.float32, math.log(0.5), math.log(4.0)))
    position = jnp.arange(TOKENS, dtype=jnp.float32)[None, :]
    envelope = jnp.exp(-rate * position / TOKENS) * jnp.sqrt(2.0 * rate / TOKENS)
    noise = jnp.clip(jax.random.normal(noise_key, (CHANNELS, TOKENS), jnp.float32), -6.0, 6.0)
    return (noise * envelope).astype(jnp.float32)


def shard_levels(stream_key, dims, pieces, smallest, largest):
    factor_of, own = 1.0, jax.random.fold_in(stream_key, 6)
    for axis_at, shards_of in pieces:
        heights = jnp.exp(jax.random.uniform(jax.random.fold_in(own, axis_at), (shards_of,), jnp.float32, smallest / len(pieces), largest / len(pieces)))
        factor_of = factor_of * jnp.repeat(heights, dims[axis_at] // shards_of).reshape([-1 if axis == axis_at else 1 for axis in range(len(dims))])
    return factor_of


def bell_draw(key, shape, width, most, cuts=(), held_as=jnp.bfloat16):
    entries = width * jax.random.normal(key, shape, jnp.float32)
    if cuts:
        entries = entries * shard_levels(key, shape, cuts, -0.22, 0.18)
    return jnp.clip(entries, -most, most).astype(held_as)


def setup_inputs(seed: int = 0) -> dict:
    keys = jax.random.split(jax.random.key(seed), 4)
    signal = bell_draw(keys[0], (CHANNELS, TOKENS), 1.0, 6.0, ((1, 256),), jnp.float32)
    filter_taps = draw_filter_taps(jax.random.fold_in(keys[3], 71), 0)
    skip_gain = bell_draw(keys[2], (CHANNELS,), 1.0, 4.0, ((0, 4),), jnp.float32)
    return dict(signal=signal, filter_taps=filter_taps, skip_gain=skip_gain)


def reference(signal, filter_taps, skip_gain):
    fft_length = 2 * TOKENS
    spectrum = jnp.fft.rfft(signal, n=fft_length, axis=1)
    filter_spectrum = jnp.fft.rfft(filter_taps, n=fft_length, axis=1)
    response = jnp.fft.irfft(spectrum * filter_spectrum, n=fft_length, axis=1)[:, :TOKENS]
    return (response + skip_gain[:, None] * signal).astype(jnp.float32)
```

```python
import functools
import math

import jax
import jax.numpy as jnp
import ml_dtypes
import numpy as np
from jax import lax
from jax.experimental import pallas as pl
from jax.experimental.pallas import tpu as pltpu
from jax.sharding import PartitionSpec as P

LENGTH = 1 << 20
BLOCKS = 256
LANES = 128
AXES = ("seq", "tp")
VMEM = pl.BlockSpec(memory_space=pltpu.VMEM)
SMEM = pl.BlockSpec(memory_space=pltpu.SMEM)
PARAMS = pltpu.CompilerParams(vmem_limit_bytes=48 * 1024 * 1024)


def device(y, z, core, x):
    return (((y % 4) * 8 + z % 8) * 2 + core) * 4 + x % 4


def member(slab, row, g):
    core = slab % 2
    y = 2 * (row // 4) + core + (g >> 2)
    z = 2 * (row % 4) + core + ((g >> 1) & 1)
    return device(y, z, core, slab + (g & 1))


def keeper(slab, row, o):
    return device(2 * (row // 4) + (o >> 2), 2 * (row % 4) + ((o >> 1) & 1), o & 1, slab)


GROUPS = [(slab, row) for slab in range(4) for row in range(8)]


def among_members(flip):
    return [(member(s, r, g), member(s, r, g ^ flip)) for s, r in GROUPS for g in range(8)]


def to_keepers(flip):
    return [(member(s, r, g), keeper(s, r, first_range(s % 2, g) ^ flip)) for s, r in GROUPS for g in range(8)]


def first_range(core, g):
    return (g & 6) | ((g & 1) ^ core)


def halves(x):
    high = x.astype(ml_dtypes.bfloat16)
    low = (x - high.astype(np.float64)).astype(ml_dtypes.bfloat16)
    return high, low


@functools.cache
def tables():
    j = np.arange(BLOCKS)[:, None]
    k = np.arange(BLOCKS)[None, :] + 0.25
    angle = 2.0 * math.pi * ((j * k) % BLOCKS) / BLOCKS
    cos, sin = np.cos(angle), np.sin(angle)
    ahead_high, ahead_low = halves(np.concatenate([cos.T, -sin.T], axis=0))
    back_high, back_low = halves(np.concatenate([cos, -sin], axis=1) / LENGTH)
    t = np.arange(4096)[:, None]
    angle = (2.0 * math.pi / LENGTH) * (t * k)
    turn = np.stack([np.cos(angle), -np.sin(angle)])
    turn = turn.reshape(2, 8, 512, BLOCKS).transpose(1, 0, 3, 2).astype(np.float32)
    b = np.arange(LANES)
    angle = 2.0 * math.pi * ((b[:, None] * b[None, :]) % LANES) / LANES
    cos, sin = np.cos(angle), np.sin(angle)
    lane_high, lane_low = halves(np.block([[cos, -sin], [sin, cos]]))
    unlane_high, unlane_low = halves(np.block([[cos, sin], [-sin, cos]]))
    angle = (2.0 * math.pi / 4096) * (np.arange(32)[:, None] * b[None, :])
    twist = np.stack([np.cos(angle), -np.sin(angle)], axis=1)
    twist = np.broadcast_to(twist[:, :, None, :], (32, 2, 8, LANES)).astype(np.float32)
    return dict(
        ahead=np.concatenate([ahead_high, ahead_high, ahead_low], axis=1),
        back=np.concatenate([back_high, back_high, back_low], axis=1),
        turn=turn,
        lane=np.concatenate([lane_high, lane_high, lane_low], axis=0),
        unlane=np.concatenate([unlane_high, unlane_high, unlane_low], axis=0),
        twist=np.ascontiguousarray(twist),
    )


def split(x):
    high = x.astype(jnp.bfloat16)
    return high, (x - high.astype(jnp.float32)).astype(jnp.bfloat16)


def dot(a, b):
    return lax.dot_general(a, b, (((1,), (0,)), ((), ())), preferred_element_type=jnp.float32)


def times(re, im, factor):
    c, s = factor.real, factor.imag
    if abs(s) < 1e-12:
        return (re, im) if c > 0 else (-re, -im)
    if abs(c) < 1e-12:
        return (-im, re) if s > 0 else (im, -re)
    if abs(abs(c) - abs(s)) < 1e-12:
        p, q = np.sign(c), np.sign(s)
        first = re - im if p == q else re + im
        second = im + re if p == q else im - re
        return first * np.float32(c), second * np.float32(c)
    c, s = np.float32(c), np.float32(s)
    return re * c - im * s, re * s + im * c


def fourier(values, sign):
    size = len(values)
    if size == 1:
        return values
    even, odd = fourier(values[0::2], sign), fourier(values[1::2], sign)
    first, second = [], []
    for i in range(size // 2):
        angle = sign * 2.0 * math.pi * i / size
        re, im = times(*odd[i], complex(math.cos(angle), math.sin(angle)))
        first.append((even[i][0] + re, even[i][1] + im))
        second.append((even[i][0] - re, even[i][1] - im))
    return first + second


def unit(sign, numerator, denominator):
    angle = sign * 2.0 * math.pi * numerator / denominator
    return complex(math.cos(angle), math.sin(angle))


def pack_kernel(signal_ref, taps_ref, out_ref, rows_ref):
    for at, ref in enumerate((signal_ref, taps_ref)):
        for cb in range(4):
            for col in range(32):
                rows_ref[at, pl.ds((cb * 32 + col) * 8, 8), :] = ref[pl.ds(8 * cb, 8), pl.ds(128 * col, 128)]
    for slab in range(4):
        for row in range(8):
            for g in range(8):
                to = member(slab, row, g)
                for at in range(2):
                    start = (slab * 32 + 4 * g) * 8 + row
                    out_ref[to, pl.ds(4 * at, 4), :] = rows_ref[at, pl.ds(start, 4, stride=8), :]


def pack(signal, taps):
    return pl.pallas_call(
        pack_kernel,
        out_shape=jax.ShapeDtypeStruct((256, 8, LANES), jnp.float32),
        in_specs=[VMEM, VMEM],
        out_specs=VMEM,
        scratch_shapes=[pltpu.VMEM((2, 1024, LANES), jnp.float32)],
        compiler_params=PARAMS,
    )(signal, taps)


def ahead_kernel(place_ref, gain_ref, x_ref, ahead_ref, turn_ref, *rest):
    outs, (x2_ref, y_ref) = rest[:8], rest[8:]
    g = place_ref[0]
    for s in range(8):
        x = x_ref[pl.ds(s, 256, stride=8), :]
        if s == 4:
            row = lax.broadcasted_iota(jnp.int32, x.shape, 0)
            lane = lax.broadcasted_iota(jnp.int32, x.shape, 1)
            x = x + jnp.where((row == 0) & (lane == 0), gain_ref[0], 0.0)
        high, low = split(x)
        x2_ref[pl.ds(0, 256), pl.ds(128 * s, 128)] = high
        x2_ref[pl.ds(256, 256), pl.ds(128 * s, 128)] = low
    for n in range(4):
        cols = pl.ds(256 * n, 256)
        y_ref[:, cols] = dot(ahead_ref[:, :512], x2_ref[:, cols]) + dot(ahead_ref[:, 512:], x2_ref[:256, cols])
    for flip in range(8):
        to = pl.multiple_of((g ^ flip) * 32, 32)
        for a in range(4):
            tr = turn_ref[0, 0, pl.ds(to, 32), pl.ds(128 * a, 128)]
            ti = turn_ref[0, 1, pl.ds(to, 32), pl.ds(128 * a, 128)]
            for sf in range(2):
                cols = pl.ds(512 * sf + 128 * a, 128)
                re, im = y_ref[pl.ds(to, 32), cols], y_ref[pl.ds(256 + to, 32), cols]
                outs[flip][0, sf, a] = re * tr - im * ti
                outs[flip][1, sf, a] = re * ti + im * tr


def whole(shape):
    return pl.BlockSpec(shape, lambda i, place: (0,) * len(shape))


def ahead(place, gain, x, table, turn):
    block = (2, 2, 4, 32, LANES)
    return pl.pallas_call(
        ahead_kernel,
        out_shape=[jax.ShapeDtypeStruct(block, jnp.float32)] * 8,
        grid_spec=pltpu.PrefetchScalarGridSpec(
            num_scalar_prefetch=1,
            grid=(1,),
            in_specs=[
                SMEM,
                whole((2048, LANES)),
                whole((512, 768)),
                pl.BlockSpec((1, 2, 256, 512), lambda i, place: (place[0], 0, 0, 0)),
            ],
            out_specs=[whole(block)] * 8,
            scratch_shapes=[pltpu.VMEM((512, 1024), jnp.bfloat16), pltpu.VMEM((512, 1024), jnp.float32)],
        ),
        compiler_params=PARAMS,
    )(place, gain, x, table, turn)


def middle_kernel(place_ref, *refs):
    ins, (lane_ref, unlane_ref, twist_ref) = refs[:8], refs[8:11]
    outs, (x_ref, m_ref, d_ref, y_ref) = refs[11:19], refs[19:]
    g, o = place_ref[0], place_ref[1]
    for flip in range(8):
        x_ref[g ^ flip] = ins[flip][...]

    def step(kb, carry):
        rows = pl.ds(pl.multiple_of(kb * 8, 8), 8)
        for sf in range(2):
            for a in range(4):
                values = [(x_ref[s, 0, sf, a, rows, :], x_ref[s, 1, sf, a, rows, :]) for s in range(8)]
                for m1, value in enumerate(fourier(values, -1)):
                    re, im = times(*value, unit(-1, a * m1, 32))
                    m_ref[m1, a, 0], m_ref[m1, a, 1] = re, im
            for m1 in range(8):
                values = fourier([(m_ref[m1, a, 0], m_ref[m1, a, 1]) for a in range(4)], -1)
                for m2, (re, im) in enumerate(values):
                    m = m1 + 8 * m2
                    tr, ti = twist_ref[m, 0], twist_ref[m, 1]
                    d_ref[pl.ds(256 * sf + 8 * m, 8), :128] = re * tr - im * ti
                    d_ref[pl.ds(256 * sf + 8 * m, 8), 128:] = re * ti + im * tr
        high, low = split(d_ref[...])
        d = dot(jnp.concatenate([high, low, high], axis=1), lane_ref[...])
        sr, si, fr, fi = d[:256, :128], d[:256, 128:], d[256:, :128], d[256:, 128:]
        high, low = split(jnp.concatenate([sr * fr - si * fi, sr * fi + si * fr], axis=1))
        d_ref[pl.ds(0, 256), :] = dot(jnp.concatenate([high, low, high], axis=1), unlane_ref[...])
        for m1 in range(8):
            values = []
            for m2 in range(4):
                m = m1 + 8 * m2
                tr, ti = twist_ref[m, 0], twist_ref[m, 1]
                re, im = d_ref[pl.ds(8 * m, 8), :128], d_ref[pl.ds(8 * m, 8), 128:]
                values.append((re * tr + im * ti, im * tr - re * ti))
            for a, value in enumerate(fourier(values, 1)):
                re, im = times(*value, unit(1, a * m1, 32))
                m_ref[m1, a, 0], m_ref[m1, a, 1] = re, im
        for a in range(4):
            values = fourier([(m_ref[m1, a, 0], m_ref[m1, a, 1]) for m1 in range(8)], 1)
            for at, (re, im) in enumerate(values):
                y_ref[at, 0, a, rows, :], y_ref[at, 1, a, rows, :] = re, im
        return carry

    lax.fori_loop(0, 4, step, 0)
    for flip in range(8):
        outs[flip][...] = y_ref[o ^ flip]


def middle(place, blocks, lane, unlane, twist):
    block = (2, 4, 32, LANES)
    return pl.pallas_call(
        middle_kernel,
        out_shape=[jax.ShapeDtypeStruct(block, jnp.float32)] * 8,
        in_specs=[SMEM] + [VMEM] * 11,
        out_specs=[VMEM] * 8,
        scratch_shapes=[
            pltpu.VMEM((8, 2, 2, 4, 32, LANES), jnp.float32),
            pltpu.VMEM((8, 4, 2, 8, LANES), jnp.float32),
            pltpu.VMEM((512, 256), jnp.float32),
            pltpu.VMEM((8, 2, 4, 32, LANES), jnp.float32),
        ],
        compiler_params=PARAMS,
    )(place, *blocks, lane, unlane, twist)


def back_kernel(place_ref, *refs):
    ins, (back_ref, turn_ref), out_ref, (y2_ref,) = refs[:8], refs[8:10], refs[10], refs[11:]
    g = place_ref[2]
    for flip in range(8):
        at = pl.multiple_of((g ^ flip) * 32, 32)
        for a in range(4):
            cols = pl.ds(128 * a, 128)
            tr, ti = turn_ref[0, 0, pl.ds(at, 32), cols], turn_ref[0, 1, pl.ds(at, 32), cols]
            re, im = ins[flip][0, a], ins[flip][1, a]
            for part, value in enumerate((re * tr + im * ti, im * tr - re * ti)):
                high, low = split(value)
                y2_ref[pl.ds(256 * part + at, 32), cols] = high
                y2_ref[pl.ds(512 + 256 * part + at, 32), cols] = low
    for n in range(2):
        cols = pl.ds(256 * n, 256)
        y = dot(back_ref[:, :1024], y2_ref[:, cols]) + dot(back_ref[:, 1024:], y2_ref[:512, cols])
        for a in range(2):
            out_ref[pl.ds(2 * n + a, 256, stride=4), :] = y[:, 128 * a : 128 * (a + 1)]


def back(place, blocks, table, turn):
    return pl.pallas_call(
        back_kernel,
        out_shape=jax.ShapeDtypeStruct((1024, LANES), jnp.float32),
        grid_spec=pltpu.PrefetchScalarGridSpec(
            num_scalar_prefetch=1,
            grid=(1,),
            in_specs=[whole((2, 4, 32, LANES))] * 8
            + [whole((256, 1536)), pl.BlockSpec((1, 2, 256, 512), lambda i, place: (place[3], 0, 0, 0))],
            out_specs=whole((1024, LANES)),
            scratch_shapes=[pltpu.VMEM((1024, 512), jnp.bfloat16)],
        ),
        compiler_params=PARAMS,
    )(place, *blocks, table, turn)


def unpack_kernel(x_ref, out_ref):
    for jl in range(4):
        for o in range(8):
            for a in range(4):
                start = (16 * (o >> 2) + 2 * ((o >> 1) & 1) + (o & 1)) * 16 + jl * 4 + a
                cols = pl.ds(128 * (jl * 32 + 4 * o + a), 128)
                for half in range(2):
                    out_ref[pl.ds(4 * half, 4), cols] = x_ref[pl.ds(start + 512 * half, 4, stride=64), :]


def unpack(x):
    return pl.pallas_call(
        unpack_kernel,
        out_shape=jax.ShapeDtypeStruct((8, 16384), jnp.float32),
        in_specs=[VMEM],
        out_specs=VMEM,
        compiler_params=PARAMS,
    )(x)


def body(signal, filter_taps, skip_gain):
    known = tables()
    seq, x = lax.axis_index("seq"), lax.axis_index("tp")
    y, z, core = seq // 16, (seq // 2) % 8, seq % 2
    dy, dz, dx = (y - core) % 2, (z - core) % 2, (x - core) % 2
    g = 4 * dy + 2 * dz + dx
    row = ((y - core) % 4) // 2 * 4 + ((z - core) % 8) // 2
    first = 4 * dy + 2 * dz + (dx ^ core)
    o = 4 * (y % 2) + 2 * (z % 2) + core
    source = 4 * (y % 2) + 2 * (z % 2) + (core ^ (x % 2))
    place = jnp.stack([g, first, source, o]).astype(jnp.int32)
    gain = jnp.where(g == 0, skip_gain[row], 0.0).reshape(1)

    packed = pack(signal, filter_taps)
    tokens = lax.all_to_all(packed, AXES, split_axis=0, concat_axis=0, tiled=True)
    turn = jnp.asarray(known["turn"])
    parts = ahead(place, gain, tokens.reshape(2048, LANES), jnp.asarray(known["ahead"]), turn)
    parts = [parts[0]] + [lax.ppermute(parts[i], AXES, among_members(i)) for i in range(1, 8)]
    parts = middle(place, parts, jnp.asarray(known["lane"]), jnp.asarray(known["unlane"]), jnp.asarray(known["twist"]))
    parts = [lax.ppermute(parts[i], AXES, to_keepers(i)) for i in range(8)]
    result = back(place, parts, jnp.asarray(known["back"]), turn)
    result = lax.all_to_all(result.reshape(64, 16, LANES), "seq", split_axis=0, concat_axis=0, tiled=True)
    return unpack(result.reshape(1024, LANES))


def solution(mesh):
    placed = (P(None, ("seq", "tp")), P(None, ("seq", "tp")), P("tp"))
    return jax.shard_map(
        body, mesh=mesh, in_specs=placed, out_specs=P("tp", "seq"), check_vma=False
    )
```

```python
import functools
import math

import jax
import jax.numpy as jnp
import ml_dtypes
import numpy as np
from jax import lax
from jax.experimental import pallas as pl
from jax.experimental.pallas import tpu as pltpu
from jax.sharding import PartitionSpec as P

LENGTH = 1 << 20
BLOCKS = 256
LANES = 128
AXES = ("seq", "tp")
FLIPS = (7, 6, 5, 3, 4, 2, 1, 0)
VMEM = pl.BlockSpec(memory_space=pltpu.VMEM)
HBM = pl.BlockSpec(memory_space=pltpu.HBM)
SMEM = pl.BlockSpec(memory_space=pltpu.SMEM)
PARAMS = pltpu.CompilerParams(vmem_limit_bytes=48 * 1024 * 1024)


def device(y, z, core, x):
    return (((y % 4) * 8 + z % 8) * 2 + core) * 4 + x % 4


def member(slab, row, g):
    core = slab % 2
    y = 2 * (row // 4) + core + (g >> 2)
    z = 2 * (row % 4) + core + ((g >> 1) & 1)
    return device(y, z, core, slab + (g & 1))


def keeper(slab, row, o):
    odd = slab % 2
    return device(2 * (row // 4) + odd + (o >> 2), 2 * (row % 4) + odd + ((o >> 1) & 1), o & 1, slab)


GROUPS = [(slab, row) for slab in range(4) for row in range(8)]


def among_members(flip):
    return [(member(s, r, g), member(s, r, g ^ flip)) for s, r in GROUPS for g in range(8)]


def to_keepers(flip):
    return [(member(s, r, g), keeper(s, r, first_range(s % 2, g) ^ flip)) for s, r in GROUPS for g in range(8)]


def first_range(core, g):
    return (g & 6) | ((g & 1) ^ core)


def halves(x):
    high = x.astype(ml_dtypes.bfloat16)
    low = (x - high.astype(np.float64)).astype(ml_dtypes.bfloat16)
    return high, low


@functools.cache
def tables():
    j = np.arange(BLOCKS)[:, None]
    k = np.arange(BLOCKS)[None, :] + 0.25
    angle = 2.0 * math.pi * ((j * k) % BLOCKS) / BLOCKS
    cos, sin = np.cos(angle), np.sin(angle)
    ahead_high, ahead_low = halves(np.concatenate([cos.T, -sin.T], axis=0))
    back_high, back_low = halves(np.concatenate([cos, -sin], axis=1) / LENGTH)
    t = np.arange(4096)[:, None]
    angle = (2.0 * math.pi / LENGTH) * (t * k)
    turn = np.stack([np.cos(angle), -np.sin(angle)])
    turn = turn.reshape(2, 8, 512, BLOCKS).transpose(1, 0, 3, 2).astype(np.float32)
    b = np.arange(LANES)
    angle = 2.0 * math.pi * ((b[:, None] * b[None, :]) % LANES) / LANES
    cos, sin = np.cos(angle), np.sin(angle)
    lane_high, lane_low = halves(np.block([[cos, -sin], [sin, cos]]))
    unlane_high, unlane_low = halves(np.block([[cos, sin], [-sin, cos]]))
    angle = (2.0 * math.pi / 4096) * (np.arange(32)[:, None] * b[None, :])
    twist = np.stack([np.cos(angle), -np.sin(angle)], axis=1)
    return dict(
        ahead=np.concatenate([ahead_high, ahead_low], axis=1),
        back=np.concatenate([back_high, back_low], axis=1),
        turn=turn,
        lane=np.concatenate([lane_high, lane_low], axis=1),
        unlane=np.concatenate([unlane_high, unlane_low], axis=1),
        twist=twist.astype(np.float32).reshape(64, LANES),
    )


def split(x):
    high = x.astype(jnp.bfloat16)
    return high, (x - high.astype(jnp.float32)).astype(jnp.bfloat16)


def dot(a, b):
    return lax.dot_general(a, b, (((1,), (0,)), ((), ())), preferred_element_type=jnp.float32)


def three(a_high, a_low, b_high, b_low):
    return dot(a_high, b_high) + (dot(a_high, b_low) + dot(a_low, b_high))


def times(re, im, factor):
    c, s = factor.real, factor.imag
    if abs(s) < 1e-12:
        return (re, im) if c > 0 else (-re, -im)
    if abs(c) < 1e-12:
        return (-im, re) if s > 0 else (im, -re)
    if abs(abs(c) - abs(s)) < 1e-12:
        p, q = np.sign(c), np.sign(s)
        first = re - im if p == q else re + im
        second = im + re if p == q else im - re
        return first * np.float32(c), second * np.float32(c)
    c, s = np.float32(c), np.float32(s)
    return re * c - im * s, re * s + im * c


def fourier(values, sign):
    size = len(values)
    if size == 1:
        return values
    even, odd = fourier(values[0::2], sign), fourier(values[1::2], sign)
    first, second = [], []
    for i in range(size // 2):
        angle = sign * 2.0 * math.pi * i / size
        re, im = times(*odd[i], complex(math.cos(angle), math.sin(angle)))
        first.append((even[i][0] + re, even[i][1] + im))
        second.append((even[i][0] - re, even[i][1] - im))
    return first + second


def unit(sign, numerator, denominator):
    angle = sign * 2.0 * math.pi * numerator / denominator
    return complex(math.cos(angle), math.sin(angle))


def pack_kernel(signal_ref, taps_ref, out_ref, rows_ref, sems):
    def load(at, ref, slab):
        rows = pl.ds(256 * slab, 256)
        return pltpu.make_async_copy(ref.at[rows, :], rows_ref.at[at, rows, :], sems.at[at, slab])

    copies = [[load(at, ref, slab) for slab in range(4)] for at, ref in enumerate((signal_ref, taps_ref))]
    for slab in range(4):
        for at in range(2):
            copies[at][slab].start()
    for slab in range(4):
        for at in range(2):
            copies[at][slab].wait()
        for row in range(8):
            for g in range(8):
                to = member(slab, row, g)
                for at in range(2):
                    start = (slab * 32 + 4 * g) * 8 + row
                    out_ref[to, pl.ds(4 * at, 4), :] = rows_ref[at, pl.ds(start, 4, stride=8), :]


def tiles(x):
    return x.reshape(4, 8, 32, LANES).swapaxes(1, 2).reshape(1024, LANES)


def pack(signal, taps):
    return pl.pallas_call(
        pack_kernel,
        out_shape=jax.ShapeDtypeStruct((256, 8, LANES), jnp.float32),
        in_specs=[HBM, HBM],
        out_specs=VMEM,
        scratch_shapes=[pltpu.VMEM((2, 1024, LANES), jnp.float32), pltpu.SemaphoreType.DMA((2, 4))],
        compiler_params=pltpu.CompilerParams(vmem_limit_bytes=60 * 1024 * 1024),
    )(tiles(signal), tiles(taps))


def turn_copies(turn_ref, at, to_ref, sems):
    parts = [(i, pl.ds(128 * h, 128)) for i in range(2) for h in range(2)]
    return [
        pltpu.make_async_copy(turn_ref.at[at, i, rows], to_ref.at[i, rows], sems.at[n])
        for n, (i, rows) in enumerate(parts)
    ]


def ahead_kernel(place_ref, gain_ref, x_ref, ahead_ref, turn_ref, *rest):
    outs, (angle_ref, x2_ref, y_ref, sems) = rest[:8], rest[8:]
    g = place_ref[0]
    copies = turn_copies(turn_ref, g, angle_ref, sems)
    for copy in copies:
        copy.start()
    for s in range(8):
        x = x_ref[pl.ds(s, 256, stride=8), :]
        if s == 4:
            row = lax.broadcasted_iota(jnp.int32, x.shape, 0)
            lane = lax.broadcasted_iota(jnp.int32, x.shape, 1)
            x = x + jnp.where((row == 0) & (lane == 0), gain_ref[0], 0.0)
        high, low = split(x)
        x2_ref[pl.ds(0, 256), pl.ds(128 * s, 128)] = high
        x2_ref[pl.ds(256, 256), pl.ds(128 * s, 128)] = low
    for n in range(4):
        cols = pl.ds(256 * n, 256)
        y_ref[:, cols] = three(ahead_ref[:, :256], ahead_ref[:, 256:], x2_ref[:256, cols], x2_ref[256:, cols])
    for copy in copies:
        copy.wait()
    for i, flip in enumerate(FLIPS):
        to = pl.multiple_of((g ^ flip) * 32, 32)
        for a in range(4):
            tr = angle_ref[0, pl.ds(to, 32), pl.ds(128 * a, 128)]
            ti = angle_ref[1, pl.ds(to, 32), pl.ds(128 * a, 128)]
            for sf in range(2):
                cols = pl.ds(512 * sf + 128 * a, 128)
                re, im = y_ref[pl.ds(to, 32), cols], y_ref[pl.ds(256 + to, 32), cols]
                outs[i][0, sf, a] = re * tr - im * ti
                outs[i][1, sf, a] = re * ti + im * tr


def ahead(place, gain, x, table, turn):
    block = (2, 2, 4, 32, LANES)
    return pl.pallas_call(
        ahead_kernel,
        out_shape=[jax.ShapeDtypeStruct(block, jnp.float32)] * 8,
        in_specs=[SMEM, SMEM, VMEM, VMEM, HBM],
        out_specs=[VMEM] * 8,
        scratch_shapes=[
            pltpu.VMEM((2, 256, 512), jnp.float32),
            pltpu.VMEM((512, 1024), jnp.bfloat16),
            pltpu.VMEM((512, 1024), jnp.float32),
            pltpu.SemaphoreType.DMA((4,)),
        ],
        compiler_params=PARAMS,
    )(place, gain, x, table, turn)


def middle_kernel(place_ref, *refs):
    ins, (lane_ref, unlane_ref, twist_ref, turn_ref) = refs[:8], refs[8:12]
    outs, angle_ref, (x_ref, m_ref, d_ref, y_ref, sems) = refs[12:20], refs[20], refs[21:]
    g, o = place_ref[0], place_ref[1]
    copies = turn_copies(turn_ref, place_ref[3], angle_ref, sems)
    for copy in copies:
        copy.start()
    for i, flip in enumerate(FLIPS):
        x_ref[g ^ flip] = ins[i][...]

    def step(kb, carry):
        rows = pl.ds(pl.multiple_of(kb * 8, 8), 8)
        for sf in range(2):
            for a in range(4):
                values = [(x_ref[s, 0, sf, a, rows, :], x_ref[s, 1, sf, a, rows, :]) for s in range(8)]
                for m1, value in enumerate(fourier(values, -1)):
                    re, im = times(*value, unit(-1, a * m1, 32))
                    m_ref[m1, a, 0], m_ref[m1, a, 1] = re, im
            for m1 in range(8):
                values = fourier([(m_ref[m1, a, 0], m_ref[m1, a, 1]) for a in range(4)], -1)
                for m2, (re, im) in enumerate(values):
                    m = m1 + 8 * m2
                    tr, ti = twist_ref[2 * m : 2 * m + 1, :], twist_ref[2 * m + 1 : 2 * m + 2, :]
                    d_ref[pl.ds(256 * sf + 8 * m, 8), :128] = re * tr - im * ti
                    d_ref[pl.ds(256 * sf + 8 * m, 8), 128:] = re * ti + im * tr
        high, low = split(d_ref[...])
        d = three(high, low, lane_ref[:, :256], lane_ref[:, 256:])
        sr, si, fr, fi = d[:256, :128], d[:256, 128:], d[256:, :128], d[256:, 128:]
        high, low = split(jnp.concatenate([sr * fr - si * fi, sr * fi + si * fr], axis=1))
        d_ref[pl.ds(0, 256), :] = three(high, low, unlane_ref[:, :256], unlane_ref[:, 256:])
        for m1 in range(8):
            values = []
            for m2 in range(4):
                m = m1 + 8 * m2
                tr, ti = twist_ref[2 * m : 2 * m + 1, :], twist_ref[2 * m + 1 : 2 * m + 2, :]
                re, im = d_ref[pl.ds(8 * m, 8), :128], d_ref[pl.ds(8 * m, 8), 128:]
                values.append((re * tr + im * ti, im * tr - re * ti))
            for a, value in enumerate(fourier(values, 1)):
                re, im = times(*value, unit(1, a * m1, 32))
                m_ref[m1, a, 0], m_ref[m1, a, 1] = re, im
        for a in range(4):
            values = fourier([(m_ref[m1, a, 0], m_ref[m1, a, 1]) for m1 in range(8)], 1)
            for at, (re, im) in enumerate(values):
                y_ref[at, 0, a, rows, :], y_ref[at, 1, a, rows, :] = re, im
        return carry

    lax.fori_loop(0, 4, step, 0)
    for i, flip in enumerate(FLIPS):
        outs[i][...] = y_ref[o ^ flip]
    for copy in copies:
        copy.wait()


def middle(place, blocks, lane, unlane, twist, turn):
    block = (2, 4, 32, LANES)
    return pl.pallas_call(
        middle_kernel,
        out_shape=[jax.ShapeDtypeStruct(block, jnp.float32)] * 8
        + [jax.ShapeDtypeStruct((2, 256, 512), jnp.float32)],
        in_specs=[SMEM] + [VMEM] * 11 + [HBM],
        out_specs=[VMEM] * 9,
        scratch_shapes=[
            pltpu.VMEM((8, 2, 2, 4, 32, LANES), jnp.float32),
            pltpu.VMEM((8, 4, 2, 8, LANES), jnp.float32),
            pltpu.VMEM((512, 256), jnp.float32),
            pltpu.VMEM((8, 2, 4, 32, LANES), jnp.float32),
            pltpu.SemaphoreType.DMA((4,)),
        ],
        compiler_params=PARAMS,
    )(place, *blocks, lane, unlane, twist, turn)


def back_kernel(place_ref, *refs):
    ins, (back_ref, turn_ref), out_ref, (y2_ref,) = refs[:8], refs[8:10], refs[10], refs[11:]
    g = place_ref[2]
    for i, flip in enumerate(FLIPS):
        at = pl.multiple_of((g ^ flip) * 32, 32)
        for a in range(4):
            cols = pl.ds(128 * a, 128)
            tr, ti = turn_ref[0, pl.ds(at, 32), cols], turn_ref[1, pl.ds(at, 32), cols]
            re, im = ins[i][0, a], ins[i][1, a]
            for part, value in enumerate((re * tr + im * ti, im * tr - re * ti)):
                high, low = split(value)
                y2_ref[pl.ds(256 * part + at, 32), cols] = high
                y2_ref[pl.ds(512 + 256 * part + at, 32), cols] = low
    for n in range(2):
        cols = pl.ds(256 * n, 256)
        y = three(back_ref[:, :512], back_ref[:, 512:], y2_ref[:512, cols], y2_ref[512:, cols])
        for a in range(2):
            out_ref[pl.ds(2 * n + a, 256, stride=4), :] = y[:, 128 * a : 128 * (a + 1)]


def back(place, blocks, table, turn):
    return pl.pallas_call(
        back_kernel,
        out_shape=jax.ShapeDtypeStruct((1024, LANES), jnp.float32),
        in_specs=[SMEM] + [VMEM] * 10,
        out_specs=VMEM,
        scratch_shapes=[pltpu.VMEM((1024, 512), jnp.bfloat16)],
        compiler_params=PARAMS,
    )(place, *blocks, table, turn)


def unpack_kernel(place_ref, x_ref, out_ref, rows_ref):
    odd = place_ref[4]
    for y in range(4):
        for z in range(8):
            start = pl.multiple_of((((y + odd) & 3) * 8 + ((z + odd) & 7)) * 32, 32)
            rows_ref[pl.ds((y * 8 + z) * 32, 32), :] = x_ref[pl.ds(start, 32), :]
    for jl in range(4):
        for o in range(8):
            for a in range(4):
                start = (16 * (o >> 2) + 2 * ((o >> 1) & 1) + (o & 1)) * 16 + jl * 4 + a
                cols = pl.ds(128 * (jl * 32 + 4 * o + a), 128)
                for half in range(2):
                    out_ref[pl.ds(4 * half, 4), cols] = rows_ref[pl.ds(start + 512 * half, 4, stride=64), :]


def unpack(place, x):
    return pl.pallas_call(
        unpack_kernel,
        out_shape=jax.ShapeDtypeStruct((8, 16384), jnp.float32),
        in_specs=[SMEM, VMEM],
        out_specs=VMEM,
        scratch_shapes=[pltpu.VMEM((1024, LANES), jnp.float32)],
        compiler_params=PARAMS,
    )(place, x)


def exchange(parts, pairs, count):
    moved = [lax.ppermute(part, AXES, pairs(flip)) for part, flip in zip(parts[:count], FLIPS)]
    return moved + list(parts[count:])


def body(signal, filter_taps, skip_gain):
    known = tables()
    seq, x = lax.axis_index("seq"), lax.axis_index("tp")
    y, z, core = seq // 16, (seq // 2) % 8, seq % 2
    dy, dz, dx = (y - core) % 2, (z - core) % 2, (x - core) % 2
    g = 4 * dy + 2 * dz + dx
    row = ((y - core) % 4) // 2 * 4 + ((z - core) % 8) // 2
    first = 4 * dy + 2 * dz + (dx ^ core)
    odd = x % 2
    o = 4 * ((y - odd) % 2) + 2 * ((z - odd) % 2) + core
    place = jnp.stack([g, first, o ^ odd, o, odd]).astype(jnp.int32)
    gain = jnp.where(g == 0, skip_gain[row], 0.0).reshape(1)

    packed = pack(signal, filter_taps)
    tokens = lax.all_to_all(packed, AXES, split_axis=0, concat_axis=0, tiled=True)
    names = ("turn", "ahead", "lane", "unlane", "twist", "back")
    turn, table, lane, unlane, twist, untable = (jnp.asarray(known[name]) for name in names)
    parts = ahead(place, gain, tokens.reshape(2048, LANES), table, turn)
    parts = exchange(parts, among_members, 7)
    *parts, turn = middle(place, parts, lane, unlane, twist, turn)
    parts = exchange(parts, to_keepers, 8)
    result = back(place, parts, untable, turn)
    result = lax.all_to_all(result.reshape(64, 16, LANES), "seq", split_axis=0, concat_axis=0, tiled=True)
    return unpack(place, result.reshape(1024, LANES))


def solution(mesh):
    placed = (P(None, ("seq", "tp")), P(None, ("seq", "tp")), P("tp"))
    return jax.shard_map(
        body, mesh=mesh, in_specs=placed, out_specs=P("tp", "seq"), check_vma=False
    )
```

```python
import functools
import math

import jax
import jax.numpy as jnp
import ml_dtypes
import numpy as np
from jax import lax
from jax.experimental import pallas as pl
from jax.experimental.pallas import tpu as pltpu
from jax.sharding import PartitionSpec as P

LENGTH = 1 << 20
BLOCKS = 256
LANES = 128
AXES = ("seq", "tp")
FLIPS = (7, 6, 5, 3, 4, 2, 1, 0)
VMEM = pl.BlockSpec(memory_space=pltpu.VMEM)
HBM = pl.BlockSpec(memory_space=pltpu.HBM)
SMEM = pl.BlockSpec(memory_space=pltpu.SMEM)
PARAMS = pltpu.CompilerParams(vmem_limit_bytes=48 * 1024 * 1024)


def device(y, z, core, x):
    return (((y % 4) * 8 + z % 8) * 2 + core) * 4 + x % 4


def member(slab, row, g):
    core = slab % 2
    y = 2 * (row // 4) + core + (g >> 2)
    z = 2 * (row % 4) + core + ((g >> 1) & 1)
    return device(y, z, core, slab + (g & 1))


def keeper(slab, row, o):
    odd = slab % 2
    return device(2 * (row // 4) + odd + (o >> 2), 2 * (row % 4) + odd + ((o >> 1) & 1), o & 1, slab)


GROUPS = [(slab, row) for slab in range(4) for row in range(8)]


def among_members(flip):
    return [(member(s, r, g), member(s, r, g ^ flip)) for s, r in GROUPS for g in range(8)]


def to_keepers(flip):
    return [(member(s, r, g), keeper(s, r, first_range(s % 2, g) ^ flip)) for s, r in GROUPS for g in range(8)]


def first_range(core, g):
    return (g & 6) | ((g & 1) ^ core)


def halves(x):
    high = x.astype(ml_dtypes.bfloat16)
    low = (x - high.astype(np.float64)).astype(ml_dtypes.bfloat16)
    return high, low


@functools.cache
def tables():
    j = np.arange(BLOCKS)[:, None]
    k = np.arange(BLOCKS)[None, :] + 0.25
    angle = 2.0 * math.pi * ((j * k) % BLOCKS) / BLOCKS
    cos, sin = np.cos(angle), np.sin(angle)
    ahead_high, ahead_low = halves(np.concatenate([cos.T, -sin.T], axis=0))
    back_high, back_low = halves(np.concatenate([cos, -sin], axis=1) / LENGTH)
    t = np.arange(4096)[:, None]
    angle = (2.0 * math.pi / LENGTH) * (t * k)
    turn = np.stack([np.cos(angle), -np.sin(angle)])
    turn = turn.reshape(2, 8, 512, BLOCKS).transpose(1, 0, 3, 2).astype(np.float32)
    b = np.arange(LANES)
    angle = 2.0 * math.pi * ((b[:, None] * b[None, :]) % LANES) / LANES
    cos, sin = np.cos(angle), np.sin(angle)
    lane_high, lane_low = halves(np.block([[cos, -sin], [sin, cos]]))
    angle = (2.0 * math.pi / 4096) * (np.arange(32)[:, None] * b[None, :])
    twist = np.stack([np.cos(angle), -np.sin(angle)], axis=1)
    return dict(
        ahead=np.stack([np.concatenate([ahead_high, ahead_low], axis=1)] * 2),
        back=np.concatenate([back_high, back_low], axis=1),
        turn=turn,
        lane=np.concatenate([lane_high, lane_low], axis=1),
        twist=twist.astype(np.float32).reshape(64, LANES),
    )


def split(x):
    high = x.astype(jnp.bfloat16)
    return high, (x - high.astype(jnp.float32)).astype(jnp.bfloat16)


def dot(a, b, side=0):
    return lax.dot_general(a, b, (((1,), (side,)), ((), ())), preferred_element_type=jnp.float32)


def three(a_high, a_low, b_high, b_low, side=0):
    return dot(a_high, b_high, side) + (dot(a_high, b_low, side) + dot(a_low, b_high, side))


def times(re, im, factor):
    c, s = factor.real, factor.imag
    if abs(s) < 1e-12:
        return (re, im) if c > 0 else (-re, -im)
    if abs(c) < 1e-12:
        return (-im, re) if s > 0 else (im, -re)
    if abs(abs(c) - abs(s)) < 1e-12:
        p, q = np.sign(c), np.sign(s)
        first = re - im if p == q else re + im
        second = im + re if p == q else im - re
        return first * np.float32(c), second * np.float32(c)
    c, s = np.float32(c), np.float32(s)
    return re * c - im * s, re * s + im * c


def fourier(values, sign):
    size = len(values)
    if size == 1:
        return values
    even, odd = fourier(values[0::2], sign), fourier(values[1::2], sign)
    first, second = [], []
    for i in range(size // 2):
        angle = sign * 2.0 * math.pi * i / size
        re, im = times(*odd[i], complex(math.cos(angle), math.sin(angle)))
        first.append((even[i][0] + re, even[i][1] + im))
        second.append((even[i][0] - re, even[i][1] - im))
    return first + second


def unit(sign, numerator, denominator):
    angle = sign * 2.0 * math.pi * numerator / denominator
    return complex(math.cos(angle), math.sin(angle))


def pack_kernel(signal_ref, taps_ref, out_ref, rows_ref, packed_ref, sems):
    def load(at, ref, slab):
        rows = pl.ds(256 * slab, 256)
        return pltpu.make_async_copy(ref.at[rows, :], rows_ref.at[at, rows, :], sems.at[at, slab])

    copies = [[load(at, ref, slab) for slab in range(4)] for at, ref in enumerate((signal_ref, taps_ref))]
    order = (0, 2, 1, 3)
    for slab in order:
        for at in range(2):
            copies[at][slab].start()
    stores = []
    for slab in order:
        for at in range(2):
            copies[at][slab].wait()
        core = slab % 2
        for row in range(8):
            for g in range(8):
                to = member(slab, row, g)
                for at in range(2):
                    start = (slab * 32 + 4 * g) * 8 + row
                    rows = rows_ref[at, pl.ds(start, 4, stride=8), :]
                    packed_ref[core, to // 8, to % 4, pl.ds(4 * at, 4), :] = rows
        if slab >= 2:
            for n in range(2):
                part = pl.ds(16 * n, 16)
                source, to = packed_ref.at[core, part], out_ref.at[part, core]
                stores.append(pltpu.make_async_copy(source, to, sems.at[2 + core, n]))
                stores[-1].start()
    for copy in stores:
        copy.wait()


def tiles(x):
    return x.reshape(4, 8, 32, LANES).swapaxes(1, 2).reshape(1024, LANES)


def pack(signal, taps):
    return pl.pallas_call(
        pack_kernel,
        out_shape=jax.ShapeDtypeStruct((32, 2, 4, 8, LANES), jnp.float32),
        in_specs=[HBM, HBM],
        out_specs=HBM,
        scratch_shapes=[
            pltpu.VMEM((2, 1024, LANES), jnp.float32),
            pltpu.VMEM((2, 32, 4, 8, LANES), jnp.float32),
            pltpu.SemaphoreType.DMA((4, 4)),
        ],
        compiler_params=pltpu.CompilerParams(vmem_limit_bytes=60 * 1024 * 1024),
    )(tiles(signal), tiles(taps))


def turn_copies(turn_ref, at, to_ref, sems):
    parts = [(i, pl.ds(128 * h, 128)) for i in range(2) for h in range(2)]
    return [
        pltpu.make_async_copy(turn_ref.at[at, i, rows], to_ref.at[i, rows], sems.at[n])
        for n, (i, rows) in enumerate(parts)
    ]


def ahead_kernel(place_ref, gain_ref, x_ref, ahead_ref, turn_ref, *rest):
    outs, (x2_ref, y_ref) = rest[:8], rest[8:]
    g = place_ref[0]
    for s in range(8):
        x = x_ref[pl.ds(s, 256, stride=8), :]
        if s == 4:
            row = lax.broadcasted_iota(jnp.int32, x.shape, 0)
            lane = lax.broadcasted_iota(jnp.int32, x.shape, 1)
            x = x + jnp.where((row == 0) & (lane == 0), gain_ref[0], 0.0)
        high, low = split(x)
        x2_ref[pl.ds(0, 256), pl.ds(128 * s, 128)] = high
        x2_ref[pl.ds(256, 256), pl.ds(128 * s, 128)] = low
    for n in range(4):
        cols = pl.ds(256 * n, 256)
        y_ref[:, cols] = three(ahead_ref[:, :256], ahead_ref[:, 256:], x2_ref[:256, cols], x2_ref[256:, cols])
    for i, flip in enumerate(FLIPS):
        to = pl.multiple_of((g ^ flip) * 32, 32)
        for a in range(4):
            tr = turn_ref[0, pl.ds(to, 32), pl.ds(128 * a, 128)]
            ti = turn_ref[1, pl.ds(to, 32), pl.ds(128 * a, 128)]
            for sf in range(2):
                cols = pl.ds(512 * sf + 128 * a, 128)
                re, im = y_ref[pl.ds(to, 32), cols], y_ref[pl.ds(256 + to, 32), cols]
                outs[i][0, sf, a] = re * tr - im * ti
                outs[i][1, sf, a] = re * ti + im * tr


def ahead(place, gain, x, table, turn):
    block = (2, 2, 4, 32, LANES)
    return pl.pallas_call(
        ahead_kernel,
        out_shape=[jax.ShapeDtypeStruct(block, jnp.float32)] * 8,
        in_specs=[SMEM, SMEM] + [VMEM] * 3,
        out_specs=[VMEM] * 8,
        scratch_shapes=[pltpu.VMEM((512, 1024), jnp.bfloat16), pltpu.VMEM((512, 1024), jnp.float32)],
        compiler_params=PARAMS,
    )(place, gain, x, table, turn)


def middle_kernel(place_ref, *refs):
    ins, (lane_ref, twist_ref, turn_ref) = refs[:8], refs[8:11]
    outs, angle_ref, (x_ref, m_ref, d_ref, y_ref, sems) = refs[11:19], refs[19], refs[20:]
    g, o = place_ref[0], place_ref[1]
    copies = turn_copies(turn_ref, place_ref[3], angle_ref, sems)
    for copy in copies:
        copy.start()
    for i, flip in enumerate(FLIPS):
        x_ref[g ^ flip] = ins[i][...]

    def step(kb, carry):
        rows = pl.ds(pl.multiple_of(kb * 8, 8), 8)
        for sf in range(2):
            for a in range(4):
                values = [(x_ref[s, 0, sf, a, rows, :], x_ref[s, 1, sf, a, rows, :]) for s in range(8)]
                for m1, value in enumerate(fourier(values, -1)):
                    re, im = times(*value, unit(-1, a * m1, 32))
                    m_ref[m1, a, 0], m_ref[m1, a, 1] = re, im
            for m1 in range(8):
                values = fourier([(m_ref[m1, a, 0], m_ref[m1, a, 1]) for a in range(4)], -1)
                for m2, (re, im) in enumerate(values):
                    m = m1 + 8 * m2
                    tr, ti = twist_ref[2 * m : 2 * m + 1, :], twist_ref[2 * m + 1 : 2 * m + 2, :]
                    d_ref[pl.ds(256 * sf + 8 * m, 8), :128] = re * tr - im * ti
                    d_ref[pl.ds(256 * sf + 8 * m, 8), 128:] = re * ti + im * tr
        high, low = split(d_ref[...])
        d = three(high, low, lane_ref[:, :256], lane_ref[:, 256:])
        sr, si, fr, fi = d[:256, :128], d[:256, 128:], d[256:, :128], d[256:, 128:]
        high, low = split(jnp.concatenate([sr * fr - si * fi, sr * fi + si * fr], axis=1))
        d_ref[pl.ds(0, 256), :] = three(high, low, lane_ref[:, :256], lane_ref[:, 256:], 1)
        for m1 in range(8):
            values = []
            for m2 in range(4):
                m = m1 + 8 * m2
                tr, ti = twist_ref[2 * m : 2 * m + 1, :], twist_ref[2 * m + 1 : 2 * m + 2, :]
                re, im = d_ref[pl.ds(8 * m, 8), :128], d_ref[pl.ds(8 * m, 8), 128:]
                values.append((re * tr + im * ti, im * tr - re * ti))
            for a, value in enumerate(fourier(values, 1)):
                re, im = times(*value, unit(1, a * m1, 32))
                m_ref[m1, a, 0], m_ref[m1, a, 1] = re, im
        for a in range(4):
            values = fourier([(m_ref[m1, a, 0], m_ref[m1, a, 1]) for m1 in range(8)], 1)
            for at, (re, im) in enumerate(values):
                y_ref[at, 0, a, rows, :], y_ref[at, 1, a, rows, :] = re, im
        return carry

    lax.fori_loop(0, 4, step, 0)
    for i, flip in enumerate(FLIPS):
        outs[i][...] = y_ref[o ^ flip]
    for copy in copies:
        copy.wait()


def middle(place, blocks, lane, twist, turn):
    block = (2, 4, 32, LANES)
    return pl.pallas_call(
        middle_kernel,
        out_shape=[jax.ShapeDtypeStruct(block, jnp.float32)] * 8
        + [jax.ShapeDtypeStruct((2, 256, 512), jnp.float32)],
        in_specs=[SMEM] + [VMEM] * 10 + [HBM],
        out_specs=[VMEM] * 9,
        scratch_shapes=[
            pltpu.VMEM((8, 2, 2, 4, 32, LANES), jnp.float32),
            pltpu.VMEM((8, 4, 2, 8, LANES), jnp.float32),
            pltpu.VMEM((512, 256), jnp.float32),
            pltpu.VMEM((8, 2, 4, 32, LANES), jnp.float32),
            pltpu.SemaphoreType.DMA((4,)),
        ],
        compiler_params=PARAMS,
    )(place, *blocks, lane, twist, turn)


def back_kernel(place_ref, *refs):
    ins, (back_ref, turn_ref), out_ref, (y2_ref,) = refs[:8], refs[8:10], refs[10], refs[11:]
    g = place_ref[2]
    for i, flip in enumerate(FLIPS):
        at = pl.multiple_of((g ^ flip) * 32, 32)
        for a in range(4):
            cols = pl.ds(128 * a, 128)
            tr, ti = turn_ref[0, pl.ds(at, 32), cols], turn_ref[1, pl.ds(at, 32), cols]
            re, im = ins[i][0, a], ins[i][1, a]
            for part, value in enumerate((re * tr + im * ti, im * tr - re * ti)):
                high, low = split(value)
                y2_ref[pl.ds(256 * part + at, 32), cols] = high
                y2_ref[pl.ds(512 + 256 * part + at, 32), cols] = low
    for n in range(2):
        cols = pl.ds(256 * n, 256)
        y = three(back_ref[:, :512], back_ref[:, 512:], y2_ref[:512, cols], y2_ref[512:, cols])
        for a in range(2):
            out_ref[pl.ds(2 * n + a, 256, stride=4), :] = y[:, 128 * a : 128 * (a + 1)]


def back(place, blocks, table, turn):
    return pl.pallas_call(
        back_kernel,
        out_shape=jax.ShapeDtypeStruct((1024, LANES), jnp.float32),
        in_specs=[SMEM] + [VMEM] * 10,
        out_specs=VMEM,
        scratch_shapes=[pltpu.VMEM((1024, 512), jnp.bfloat16)],
        compiler_params=PARAMS,
    )(place, *blocks, table, turn)


def unpack_kernel(place_ref, x_ref, out_ref, rows_ref, block_ref, sems):
    odd = place_ref[4]
    for y in range(4):
        for z in range(8):
            start = pl.multiple_of((((y + odd) & 3) * 8 + ((z + odd) & 7)) * 32, 32)
            rows_ref[pl.ds((y * 8 + z) * 32, 32), :] = x_ref[pl.ds(start, 32), :]
    copies = []
    for jl in range(4):
        for o in range(8):
            for a in range(4):
                start = (16 * (o >> 2) + 2 * ((o >> 1) & 1) + (o & 1)) * 16 + jl * 4 + a
                cols = pl.ds(128 * (4 * o + a), 128)
                for half in range(2):
                    rows = rows_ref[pl.ds(start + 512 * half, 4, stride=64), :]
                    block_ref[jl, pl.ds(4 * half, 4), cols] = rows
        copies.append(pltpu.make_async_copy(block_ref.at[jl], out_ref.at[:, pl.ds(4096 * jl, 4096)], sems.at[jl]))
        copies[-1].start()
    for copy in copies:
        copy.wait()


def unpack(place, x):
    return pl.pallas_call(
        unpack_kernel,
        out_shape=jax.ShapeDtypeStruct((8, 16384), jnp.float32),
        in_specs=[SMEM, VMEM],
        out_specs=HBM,
        scratch_shapes=[
            pltpu.VMEM((1024, LANES), jnp.float32),
            pltpu.VMEM((4, 8, 4096), jnp.float32),
            pltpu.SemaphoreType.DMA((4,)),
        ],
        compiler_params=PARAMS,
    )(place, x)


def exchange(parts, pairs, count):
    moved = [lax.ppermute(part, AXES, pairs(flip)) for part, flip in zip(parts[:count], FLIPS)]
    return moved + list(parts[count:])


def body(signal, filter_taps, skip_gain):
    known = tables()
    seq, x = lax.axis_index("seq"), lax.axis_index("tp")
    y, z, core = seq // 16, (seq // 2) % 8, seq % 2
    dy, dz, dx = (y - core) % 2, (z - core) % 2, (x - core) % 2
    g = 4 * dy + 2 * dz + dx
    row = ((y - core) % 4) // 2 * 4 + ((z - core) % 8) // 2
    first = 4 * dy + 2 * dz + (dx ^ core)
    odd = x % 2
    o = 4 * ((y - odd) % 2) + 2 * ((z - odd) % 2) + core
    place = jnp.stack([g, first, o ^ odd, o, odd]).astype(jnp.int32)
    gain = jnp.where(g == 0, skip_gain[row], 0.0).reshape(1)

    packed = pack(signal, filter_taps).reshape(256, 8, LANES)
    tokens = lax.all_to_all(packed, AXES, split_axis=0, concat_axis=0, tiled=True)
    names = ("turn", "ahead", "lane", "twist", "back")
    turn, table, lane, twist, untable = (jnp.asarray(known[name]) for name in names)
    table = lax.dynamic_index_in_dim(table, core, keepdims=False)
    turn_in = lax.dynamic_index_in_dim(turn, g, keepdims=False)
    parts = ahead(place, gain, tokens.reshape(2048, LANES), table, turn_in)
    parts = exchange(parts, among_members, 7)
    *parts, turn = middle(place, parts, lane, twist, turn)
    parts = exchange(parts, to_keepers, 8)
    result = back(place, parts, untable, turn)
    result = lax.all_to_all(result.reshape(64, 16, LANES), "seq", split_axis=0, concat_axis=0, tiled=True)
    return unpack(place, result.reshape(1024, LANES))


def solution(mesh):
    placed = (P(None, ("seq", "tp")), P(None, ("seq", "tp")), P("tp"))
    return jax.shard_map(
        body, mesh=mesh, in_specs=placed, out_specs=P("tp", "seq"), check_vma=False
    )
```

```python
import functools
import math

import jax
import jax.numpy as jnp
import ml_dtypes
import numpy as np
from jax import lax
from jax.experimental import pallas as pl
from jax.experimental.pallas import tpu as pltpu
from jax.sharding import PartitionSpec as P

LENGTH = 1 << 20
BLOCKS = 256
LANES = 128
AXES = ("seq", "tp")
FLIPS = (7, 6, 5, 3, 4, 2, 1, 0)
VMEM = pl.BlockSpec(memory_space=pltpu.VMEM)
HBM = pl.BlockSpec(memory_space=pltpu.HBM)
SMEM = pl.BlockSpec(memory_space=pltpu.SMEM)
PARAMS = pltpu.CompilerParams(vmem_limit_bytes=48 * 1024 * 1024)


def device(y, z, core, x):
    return (((y % 4) * 8 + z % 8) * 2 + core) * 4 + x % 4


def member(slab, row, g):
    core = slab % 2
    y = 2 * (row // 4) + core + (g >> 2)
    z = 2 * (row % 4) + core + ((g >> 1) & 1)
    return device(y, z, core, slab + (g & 1))


def keeper(slab, row, o):
    odd = slab % 2
    return device(2 * (row // 4) + odd + (o >> 2), 2 * (row % 4) + odd + ((o >> 1) & 1), o & 1, slab)


GROUPS = [(slab, row) for slab in range(4) for row in range(8)]


def among_members(flip):
    return [(member(s, r, g), member(s, r, g ^ flip)) for s, r in GROUPS for g in range(8)]


def to_keepers(flip):
    return [(member(s, r, g), keeper(s, r, first_range(s % 2, g) ^ flip)) for s, r in GROUPS for g in range(8)]


def first_range(core, g):
    return (g & 6) | ((g & 1) ^ core)


def halves(x):
    high = x.astype(ml_dtypes.bfloat16)
    low = (x - high.astype(np.float64)).astype(ml_dtypes.bfloat16)
    return high, low


@functools.cache
def tables():
    j = np.arange(BLOCKS)[:, None]
    k = np.arange(BLOCKS)[None, :] + 0.25
    angle = 2.0 * math.pi * ((j * k) % BLOCKS) / BLOCKS
    cos, sin = np.cos(angle), np.sin(angle)
    ahead_high, ahead_low = halves(np.concatenate([cos.T, -sin.T], axis=0))
    back_high, back_low = halves(np.concatenate([cos, -sin], axis=1) / LENGTH)
    t = np.arange(4096)[:, None]
    angle = (2.0 * math.pi / LENGTH) * (t * k)
    turn = np.stack([np.cos(angle), -np.sin(angle)])
    turn = turn.reshape(2, 8, 512, BLOCKS).transpose(1, 0, 3, 2).astype(np.float32)
    b = np.arange(LANES)
    angle = 2.0 * math.pi * ((b[:, None] * b[None, :]) % LANES) / LANES
    cos, sin = np.cos(angle), np.sin(angle)
    lane_high, lane_low = halves(np.block([[cos, -sin], [sin, cos]]))
    angle = (2.0 * math.pi / 4096) * (np.arange(32)[:, None] * b[None, :])
    twist = np.stack([np.cos(angle), -np.sin(angle)], axis=1)
    return dict(
        ahead=np.stack([np.concatenate([ahead_high, ahead_low], axis=1)] * 2),
        back=np.concatenate([back_high, back_low], axis=1),
        turn=turn,
        lane=np.concatenate([lane_high, lane_low], axis=1),
        twist=twist.astype(np.float32).reshape(64, LANES),
    )


def split(x):
    high = x.astype(jnp.bfloat16)
    return high, (x - high.astype(jnp.float32)).astype(jnp.bfloat16)


def dot(a, b, side=0):
    return lax.dot_general(a, b, (((1,), (side,)), ((), ())), preferred_element_type=jnp.float32)


def three(a_high, a_low, b_high, b_low, side=0):
    return dot(a_high, b_high, side) + (dot(a_high, b_low, side) + dot(a_low, b_high, side))


def times(re, im, factor):
    c, s = factor.real, factor.imag
    if abs(s) < 1e-12:
        return (re, im) if c > 0 else (-re, -im)
    if abs(c) < 1e-12:
        return (-im, re) if s > 0 else (im, -re)
    if abs(abs(c) - abs(s)) < 1e-12:
        p, q = np.sign(c), np.sign(s)
        first = re - im if p == q else re + im
        second = im + re if p == q else im - re
        return first * np.float32(c), second * np.float32(c)
    c, s = np.float32(c), np.float32(s)
    return re * c - im * s, re * s + im * c


def fourier(values, sign):
    size = len(values)
    if size == 1:
        return values
    even, odd = fourier(values[0::2], sign), fourier(values[1::2], sign)
    first, second = [], []
    for i in range(size // 2):
        angle = sign * 2.0 * math.pi * i / size
        re, im = times(*odd[i], complex(math.cos(angle), math.sin(angle)))
        first.append((even[i][0] + re, even[i][1] + im))
        second.append((even[i][0] - re, even[i][1] - im))
    return first + second


def unit(sign, numerator, denominator):
    angle = sign * 2.0 * math.pi * numerator / denominator
    return complex(math.cos(angle), math.sin(angle))


def pack_kernel(signal_ref, taps_ref, out_ref, rows_ref, packed_ref, sems):
    def load(at, ref, slab):
        rows = pl.ds(256 * slab, 256)
        return pltpu.make_async_copy(ref.at[rows, :], rows_ref.at[at, rows, :], sems.at[at, slab])

    copies = [[load(at, ref, slab) for slab in range(4)] for at, ref in enumerate((signal_ref, taps_ref))]
    order = (0, 2, 1, 3)
    for slab in order:
        for at in range(2):
            copies[at][slab].start()
    stores = []
    for slab in order:
        for at in range(2):
            copies[at][slab].wait()
        core = slab % 2
        for row in range(8):
            for g in range(8):
                to = member(slab, row, g)
                for at in range(2):
                    start = (slab * 32 + 4 * g) * 8 + row
                    rows = rows_ref[at, pl.ds(start, 4, stride=8), :]
                    packed_ref[core, to // 8, to % 4, pl.ds(4 * at, 4), :] = rows
        if slab >= 2:
            for n in range(2):
                part = pl.ds(16 * n, 16)
                source, to = packed_ref.at[core, part], out_ref.at[part, core]
                stores.append(pltpu.make_async_copy(source, to, sems.at[2 + core, n]))
                stores[-1].start()
    for copy in stores:
        copy.wait()


def tiles(x):
    return x.reshape(4, 8, 32, LANES).swapaxes(1, 2).reshape(1024, LANES)


def pack(signal, taps):
    return pl.pallas_call(
        pack_kernel,
        out_shape=jax.ShapeDtypeStruct((32, 2, 4, 8, LANES), jnp.float32),
        in_specs=[HBM, HBM],
        out_specs=HBM,
        scratch_shapes=[
            pltpu.VMEM((2, 1024, LANES), jnp.float32),
            pltpu.VMEM((2, 32, 4, 8, LANES), jnp.float32),
            pltpu.SemaphoreType.DMA((4, 4)),
        ],
        compiler_params=pltpu.CompilerParams(vmem_limit_bytes=60 * 1024 * 1024),
    )(tiles(signal), tiles(taps))


def turn_copies(turn_ref, at, to_ref, sems):
    parts = [(i, pl.ds(128 * h, 128)) for i in range(2) for h in range(2)]
    return [
        pltpu.make_async_copy(turn_ref.at[at, i, rows], to_ref.at[i, rows], sems.at[n])
        for n, (i, rows) in enumerate(parts)
    ]


def ahead_kernel(place_ref, gain_ref, x_ref, ahead_ref, turn_ref, *rest):
    outs, (x2_ref, y_ref) = rest[:8], rest[8:]
    g = place_ref[0]
    for s in range(8):
        x = x_ref[pl.ds(s, 256, stride=8), :]
        if s == 4:
            row = lax.broadcasted_iota(jnp.int32, x.shape, 0)
            lane = lax.broadcasted_iota(jnp.int32, x.shape, 1)
            x = x + jnp.where((row == 0) & (lane == 0), gain_ref[0], 0.0)
        high, low = split(x)
        x2_ref[pl.ds(0, 256), pl.ds(128 * s, 128)] = high
        x2_ref[pl.ds(256, 256), pl.ds(128 * s, 128)] = low
    for n in range(4):
        cols = pl.ds(256 * n, 256)
        y_ref[:, cols] = three(ahead_ref[:, :256], ahead_ref[:, 256:], x2_ref[:256, cols], x2_ref[256:, cols])
    for i, flip in enumerate(FLIPS):
        to = pl.multiple_of((g ^ flip) * 32, 32)
        for a in range(4):
            tr = turn_ref[0, pl.ds(to, 32), pl.ds(128 * a, 128)]
            ti = turn_ref[1, pl.ds(to, 32), pl.ds(128 * a, 128)]
            for sf in range(2):
                cols = pl.ds(512 * sf + 128 * a, 128)
                re, im = y_ref[pl.ds(to, 32), cols], y_ref[pl.ds(256 + to, 32), cols]
                outs[i][0, sf, a] = re * tr - im * ti
                outs[i][1, sf, a] = re * ti + im * tr


def ahead(place, gain, x, table, turn):
    block = (2, 2, 4, 32, LANES)
    return pl.pallas_call(
        ahead_kernel,
        out_shape=[jax.ShapeDtypeStruct(block, jnp.float32)] * 8,
        in_specs=[SMEM, SMEM] + [VMEM] * 3,
        out_specs=[VMEM] * 8,
        scratch_shapes=[pltpu.VMEM((512, 1024), jnp.bfloat16), pltpu.VMEM((512, 1024), jnp.float32)],
        compiler_params=PARAMS,
    )(place, gain, x, table, turn)


def middle_kernel(place_ref, *refs):
    ins, (lane_ref, twist_ref, turn_ref) = refs[:8], refs[8:11]
    outs, angle_ref, (x_ref, m_ref, d_ref, y_ref, sems) = refs[11:19], refs[19], refs[20:]
    g, o = place_ref[0], place_ref[1]
    copies = turn_copies(turn_ref, place_ref[3], angle_ref, sems)
    for copy in copies:
        copy.start()
    for i, flip in enumerate(FLIPS):
        x_ref[g ^ flip] = ins[i][...]

    def step(kb, carry):
        rows = pl.ds(pl.multiple_of(kb * 16, 16), 16)
        for sf in range(2):
            for a in range(4):
                values = [(x_ref[s, 0, sf, a, rows, :], x_ref[s, 1, sf, a, rows, :]) for s in range(8)]
                for m1, value in enumerate(fourier(values, -1)):
                    re, im = times(*value, unit(-1, a * m1, 32))
                    m_ref[m1, a, 0], m_ref[m1, a, 1] = re, im
            for m1 in range(8):
                values = fourier([(m_ref[m1, a, 0], m_ref[m1, a, 1]) for a in range(4)], -1)
                for m2, (re, im) in enumerate(values):
                    m = m1 + 8 * m2
                    tr, ti = twist_ref[2 * m : 2 * m + 1, :], twist_ref[2 * m + 1 : 2 * m + 2, :]
                    d_ref[pl.ds(512 * sf + 16 * m, 16), :128] = re * tr - im * ti
                    d_ref[pl.ds(512 * sf + 16 * m, 16), 128:] = re * ti + im * tr
        high, low = split(d_ref[...])
        d = three(high, low, lane_ref[:, :256], lane_ref[:, 256:])
        sr, si, fr, fi = d[:512, :128], d[:512, 128:], d[512:, :128], d[512:, 128:]
        high, low = split(jnp.concatenate([sr * fr - si * fi, sr * fi + si * fr], axis=1))
        d_ref[pl.ds(0, 512), :] = three(high, low, lane_ref[:, :256], lane_ref[:, 256:], 1)
        for m1 in range(8):
            values = []
            for m2 in range(4):
                m = m1 + 8 * m2
                tr, ti = twist_ref[2 * m : 2 * m + 1, :], twist_ref[2 * m + 1 : 2 * m + 2, :]
                re, im = d_ref[pl.ds(16 * m, 16), :128], d_ref[pl.ds(16 * m, 16), 128:]
                values.append((re * tr + im * ti, im * tr - re * ti))
            for a, value in enumerate(fourier(values, 1)):
                re, im = times(*value, unit(1, a * m1, 32))
                m_ref[m1, a, 0], m_ref[m1, a, 1] = re, im
        for a in range(4):
            values = fourier([(m_ref[m1, a, 0], m_ref[m1, a, 1]) for m1 in range(8)], 1)
            for at, (re, im) in enumerate(values):
                y_ref[at, 0, a, rows, :], y_ref[at, 1, a, rows, :] = re, im
        return carry

    lax.fori_loop(0, 2, step, 0)
    for i, flip in enumerate(FLIPS):
        outs[i][...] = y_ref[o ^ flip]
    for copy in copies:
        copy.wait()


def middle(place, blocks, lane, twist, turn):
    block = (2, 4, 32, LANES)
    return pl.pallas_call(
        middle_kernel,
        out_shape=[jax.ShapeDtypeStruct(block, jnp.float32)] * 8
        + [jax.ShapeDtypeStruct((2, 256, 512), jnp.float32)],
        in_specs=[SMEM] + [VMEM] * 10 + [HBM],
        out_specs=[VMEM] * 9,
        scratch_shapes=[
            pltpu.VMEM((8, 2, 2, 4, 32, LANES), jnp.float32),
            pltpu.VMEM((8, 4, 2, 16, LANES), jnp.float32),
            pltpu.VMEM((1024, 256), jnp.float32),
            pltpu.VMEM((8, 2, 4, 32, LANES), jnp.float32),
            pltpu.SemaphoreType.DMA((4,)),
        ],
        compiler_params=PARAMS,
    )(place, *blocks, lane, twist, turn)


def back_kernel(place_ref, *refs):
    ins, (back_ref, turn_ref), out_ref, (y2_ref,) = refs[:8], refs[8:10], refs[10], refs[11:]
    g = place_ref[2]
    for i, flip in enumerate(FLIPS):
        at = pl.multiple_of((g ^ flip) * 32, 32)
        for a in range(4):
            cols = pl.ds(128 * a, 128)
            tr, ti = turn_ref[0, pl.ds(at, 32), cols], turn_ref[1, pl.ds(at, 32), cols]
            re, im = ins[i][0, a], ins[i][1, a]
            for part, value in enumerate((re * tr + im * ti, im * tr - re * ti)):
                high, low = split(value)
                y2_ref[pl.ds(256 * part + at, 32), cols] = high
                y2_ref[pl.ds(512 + 256 * part + at, 32), cols] = low
    for n in range(2):
        cols = pl.ds(256 * n, 256)
        y = three(back_ref[:, :512], back_ref[:, 512:], y2_ref[:512, cols], y2_ref[512:, cols])
        for a in range(2):
            out_ref[pl.ds(2 * n + a, 256, stride=4), :] = y[:, 128 * a : 128 * (a + 1)]


def back(place, blocks, table, turn):
    return pl.pallas_call(
        back_kernel,
        out_shape=jax.ShapeDtypeStruct((1024, LANES), jnp.float32),
        in_specs=[SMEM] + [VMEM] * 10,
        out_specs=VMEM,
        scratch_shapes=[pltpu.VMEM((1024, 512), jnp.bfloat16)],
        compiler_params=PARAMS,
    )(place, *blocks, table, turn)


def unpack_kernel(place_ref, x_ref, out_ref, rows_ref, block_ref, sems):
    odd = place_ref[4]
    for o in range(4):
        for row in range(8):
            y, z = 2 * (row >> 2) + (o >> 1), 2 * (row & 3) + (o & 1)
            start = pl.multiple_of((((y + odd) & 3) * 8 + ((z + odd) & 7)) * 32, 32)
            rows_ref[pl.ds((o * 8 + row) * 32, 32), :] = x_ref[pl.ds(start, 32), :]
    copies = []
    for jl in range(4):
        for o in range(8):
            for a in range(4):
                start = (o >> 1) * 256 + (o & 1) * 16 + jl * 4 + a
                block_ref[jl, :, pl.ds(128 * (4 * o + a), 128)] = rows_ref[pl.ds(start, 8, stride=32), :]
        copies.append(pltpu.make_async_copy(block_ref.at[jl], out_ref.at[:, pl.ds(4096 * jl, 4096)], sems.at[jl]))
        copies[-1].start()
    for copy in copies:
        copy.wait()


def unpack(place, x):
    return pl.pallas_call(
        unpack_kernel,
        out_shape=jax.ShapeDtypeStruct((8, 16384), jnp.float32),
        in_specs=[SMEM, VMEM],
        out_specs=HBM,
        scratch_shapes=[
            pltpu.VMEM((1024, LANES), jnp.float32),
            pltpu.VMEM((4, 8, 4096), jnp.float32),
            pltpu.SemaphoreType.DMA((4,)),
        ],
        compiler_params=PARAMS,
    )(place, x)


def exchange(parts, pairs, count):
    moved = [lax.ppermute(part, AXES, pairs(flip)) for part, flip in zip(parts[:count], FLIPS)]
    return moved + list(parts[count:])


def body(signal, filter_taps, skip_gain):
    known = tables()
    seq, x = lax.axis_index("seq"), lax.axis_index("tp")
    y, z, core = seq // 16, (seq // 2) % 8, seq % 2
    dy, dz, dx = (y - core) % 2, (z - core) % 2, (x - core) % 2
    g = 4 * dy + 2 * dz + dx
    row = ((y - core) % 4) // 2 * 4 + ((z - core) % 8) // 2
    first = 4 * dy + 2 * dz + (dx ^ core)
    odd = x % 2
    o = 4 * ((y - odd) % 2) + 2 * ((z - odd) % 2) + core
    place = jnp.stack([g, first, o ^ odd, o, odd]).astype(jnp.int32)
    gain = jnp.where(g == 0, skip_gain[row], 0.0).reshape(1)

    packed = pack(signal, filter_taps).reshape(256, 8, LANES)
    tokens = lax.all_to_all(packed, AXES, split_axis=0, concat_axis=0, tiled=True)
    names = ("turn", "ahead", "lane", "twist", "back")
    turn, table, lane, twist, untable = (jnp.asarray(known[name]) for name in names)
    table = lax.dynamic_index_in_dim(table, core, keepdims=False)
    turn_in = lax.dynamic_index_in_dim(turn, g, keepdims=False)
    parts = ahead(place, gain, tokens.reshape(2048, LANES), table, turn_in)
    parts = exchange(parts, among_members, 7)
    *parts, turn = middle(place, parts, lane, twist, turn)
    parts = exchange(parts, to_keepers, 8)
    result = back(place, parts, untable, turn)
    result = lax.all_to_all(result.reshape(64, 16, LANES), "seq", split_axis=0, concat_axis=0, tiled=True)
    return unpack(place, result.reshape(1024, LANES))


def solution(mesh):
    placed = (P(None, ("seq", "tp")), P(None, ("seq", "tp")), P("tp"))
    return jax.shard_map(
        body, mesh=mesh, in_specs=placed, out_specs=P("tp", "seq"), check_vma=False
    )
```

```python
import functools
import math

import jax
import jax.numpy as jnp
import ml_dtypes
import numpy as np
from jax import lax
from jax.experimental import pallas as pl
from jax.experimental.pallas import tpu as pltpu
from jax.sharding import PartitionSpec as P

LENGTH = 1 << 20
BLOCKS = 256
LANES = 128
AXES = ("seq", "tp")
FLIPS = (7, 6, 5, 3, 4, 2, 1, 0)
BACK_FLIPS = (6, 7, 4, 5, 2, 3, 0, 1)
VMEM = pl.BlockSpec(memory_space=pltpu.VMEM)
HBM = pl.BlockSpec(memory_space=pltpu.HBM)
SMEM = pl.BlockSpec(memory_space=pltpu.SMEM)
PARAMS = pltpu.CompilerParams(vmem_limit_bytes=48 * 1024 * 1024)


def device(y, z, core, x):
    return (((y % 4) * 8 + z % 8) * 2 + core) * 4 + x % 4


def member(slab, row, g):
    core = slab % 2
    y = 2 * (row // 4) + core + (g >> 2)
    z = 2 * (row % 4) + core + ((g >> 1) & 1)
    return device(y, z, core, slab + (g & 1))


def keeper(slab, row, o):
    odd = slab % 2
    return device(2 * (row // 4) + odd + (o >> 2), 2 * (row % 4) + odd + ((o >> 1) & 1), o & 1, slab)


GROUPS = [(slab, row) for slab in range(4) for row in range(8)]


def among_members(flip):
    return [(member(s, r, g), member(s, r, g ^ flip)) for s, r in GROUPS for g in range(8)]


def to_keepers(flip):
    return [(member(s, r, g), keeper(s, r, first_range(s % 2, g) ^ flip)) for s, r in GROUPS for g in range(8)]


def first_range(core, g):
    return (g & 6) | ((g & 1) ^ core)


def halves(x):
    high = x.astype(ml_dtypes.bfloat16)
    low = (x - high.astype(np.float64)).astype(ml_dtypes.bfloat16)
    return high, low


@functools.cache
def tables():
    j = np.arange(BLOCKS)[:, None]
    k = np.arange(BLOCKS)[None, :] + 0.25
    angle = 2.0 * math.pi * ((j * k) % BLOCKS) / BLOCKS
    cos, sin = np.cos(angle), np.sin(angle)
    ahead_high, ahead_low = halves(np.concatenate([cos.T, -sin.T], axis=0))
    back_high, back_low = halves(np.concatenate([cos, -sin], axis=1) / LENGTH)
    t = np.arange(4096)[:, None]
    angle = (2.0 * math.pi / LENGTH) * (t * k)
    turn = np.stack([np.cos(angle), -np.sin(angle)])
    turn = turn.reshape(2, 8, 512, BLOCKS).transpose(1, 0, 3, 2).astype(np.float32)
    b = np.arange(LANES)
    angle = 2.0 * math.pi * ((b[:, None] * b[None, :]) % LANES) / LANES
    cos, sin = np.cos(angle), np.sin(angle)
    lane_high, lane_low = halves(np.block([[cos, -sin], [sin, cos]]))
    angle = (2.0 * math.pi / 4096) * (np.arange(32)[:, None] * b[None, :])
    twist = np.stack([np.cos(angle), -np.sin(angle)], axis=1)
    return dict(
        ahead=np.stack([np.concatenate([ahead_high, ahead_low], axis=1)] * 2),
        back=np.concatenate([back_high, back_low], axis=1),
        turn=turn,
        lane=np.concatenate([lane_high, lane_low], axis=1),
        twist=twist.astype(np.float32).reshape(64, LANES),
    )


def split(x):
    high = x.astype(jnp.bfloat16)
    return high, (x - high.astype(jnp.float32)).astype(jnp.bfloat16)


def dot(a, b, side=0):
    return lax.dot_general(a, b, (((1,), (side,)), ((), ())), preferred_element_type=jnp.float32)


def three(a_high, a_low, b_high, b_low, side=0):
    return dot(a_high, b_high, side) + (dot(a_high, b_low, side) + dot(a_low, b_high, side))


def times(re, im, factor):
    c, s = factor.real, factor.imag
    if abs(s) < 1e-12:
        return (re, im) if c > 0 else (-re, -im)
    if abs(c) < 1e-12:
        return (-im, re) if s > 0 else (im, -re)
    if abs(abs(c) - abs(s)) < 1e-12:
        p, q = np.sign(c), np.sign(s)
        first = re - im if p == q else re + im
        second = im + re if p == q else im - re
        return first * np.float32(c), second * np.float32(c)
    c, s = np.float32(c), np.float32(s)
    return re * c - im * s, re * s + im * c


def fourier(values, sign):
    size = len(values)
    if size == 1:
        return values
    even, odd = fourier(values[0::2], sign), fourier(values[1::2], sign)
    first, second = [], []
    for i in range(size // 2):
        angle = sign * 2.0 * math.pi * i / size
        re, im = times(*odd[i], complex(math.cos(angle), math.sin(angle)))
        first.append((even[i][0] + re, even[i][1] + im))
        second.append((even[i][0] - re, even[i][1] - im))
    return first + second


def unit(sign, numerator, denominator):
    angle = sign * 2.0 * math.pi * numerator / denominator
    return complex(math.cos(angle), math.sin(angle))


def pack_kernel(signal_ref, taps_ref, out_ref, rows_ref, packed_ref, sems):
    def load(at, ref, slab):
        rows = pl.ds(256 * slab, 256)
        return pltpu.make_async_copy(ref.at[rows, :], rows_ref.at[at, rows, :], sems.at[at, slab])

    copies = [[load(at, ref, slab) for slab in range(4)] for at, ref in enumerate((signal_ref, taps_ref))]
    order = (0, 2, 1, 3)
    for slab in order:
        for at in range(2):
            copies[at][slab].start()
    stores = []
    for slab in order:
        for at in range(2):
            copies[at][slab].wait()
        core = slab % 2
        for row in range(8):
            for g in range(8):
                to = member(slab, row, g)
                for at in range(2):
                    start = (slab * 32 + 4 * g) * 8 + row
                    rows = rows_ref[at, pl.ds(start, 4, stride=8), :]
                    packed_ref[core, to // 8, to % 4, pl.ds(4 * at, 4), :] = rows
        if slab >= 2:
            for n in range(2):
                part = pl.ds(16 * n, 16)
                source, to = packed_ref.at[core, part], out_ref.at[part, core]
                stores.append(pltpu.make_async_copy(source, to, sems.at[2 + core, n]))
                stores[-1].start()
    for copy in stores:
        copy.wait()


def tiles(x):
    return x.reshape(4, 8, 32, LANES).swapaxes(1, 2).reshape(1024, LANES)


def pack(signal, taps):
    return pl.pallas_call(
        pack_kernel,
        out_shape=jax.ShapeDtypeStruct((32, 2, 4, 8, LANES), jnp.float32),
        in_specs=[HBM, HBM],
        out_specs=HBM,
        scratch_shapes=[
            pltpu.VMEM((2, 1024, LANES), jnp.float32),
            pltpu.VMEM((2, 32, 4, 8, LANES), jnp.float32),
            pltpu.SemaphoreType.DMA((4, 4)),
        ],
        compiler_params=pltpu.CompilerParams(vmem_limit_bytes=60 * 1024 * 1024),
    )(tiles(signal), tiles(taps))


def turn_copies(turn_ref, at, to_ref, sems):
    parts = [(i, pl.ds(128 * h, 128)) for i in range(2) for h in range(2)]
    return [
        pltpu.make_async_copy(turn_ref.at[at, i, rows], to_ref.at[i, rows], sems.at[n])
        for n, (i, rows) in enumerate(parts)
    ]


def ahead_kernel(place_ref, gain_ref, x_ref, ahead_ref, turn_ref, *rest):
    outs, (x2_ref, y_ref) = rest[:8], rest[8:]
    g = place_ref[0]
    for s in range(8):
        x = x_ref[pl.ds(s, 256, stride=8), :]
        if s == 4:
            row = lax.broadcasted_iota(jnp.int32, x.shape, 0)
            lane = lax.broadcasted_iota(jnp.int32, x.shape, 1)
            x = x + jnp.where((row == 0) & (lane == 0), gain_ref[0], 0.0)
        high, low = split(x)
        x2_ref[pl.ds(0, 256), pl.ds(128 * s, 128)] = high
        x2_ref[pl.ds(256, 256), pl.ds(128 * s, 128)] = low
    for n in range(4):
        cols = pl.ds(256 * n, 256)
        y_ref[:, cols] = three(ahead_ref[:, :256], ahead_ref[:, 256:], x2_ref[:256, cols], x2_ref[256:, cols])
    for i, flip in enumerate(FLIPS):
        to = pl.multiple_of((g ^ flip) * 32, 32)
        for a in range(4):
            tr = turn_ref[0, pl.ds(to, 32), pl.ds(128 * a, 128)]
            ti = turn_ref[1, pl.ds(to, 32), pl.ds(128 * a, 128)]
            for sf in range(2):
                cols = pl.ds(512 * sf + 128 * a, 128)
                re, im = y_ref[pl.ds(to, 32), cols], y_ref[pl.ds(256 + to, 32), cols]
                outs[i][0, sf, a] = re * tr - im * ti
                outs[i][1, sf, a] = re * ti + im * tr


def ahead(place, gain, x, table, turn):
    block = (2, 2, 4, 32, LANES)
    return pl.pallas_call(
        ahead_kernel,
        out_shape=[jax.ShapeDtypeStruct(block, jnp.float32)] * 8,
        in_specs=[SMEM, SMEM] + [VMEM] * 3,
        out_specs=[VMEM] * 8,
        scratch_shapes=[pltpu.VMEM((512, 1024), jnp.bfloat16), pltpu.VMEM((512, 1024), jnp.float32)],
        compiler_params=PARAMS,
    )(place, gain, x, table, turn)


def middle_kernel(place_ref, *refs):
    ins, (lane_ref, twist_ref, turn_ref) = refs[:8], refs[8:11]
    outs, angle_ref, (x_ref, m_ref, d_ref, y_ref, sems) = refs[11:19], refs[19], refs[20:]
    g, o = place_ref[0], place_ref[1]
    copies = turn_copies(turn_ref, place_ref[3], angle_ref, sems)
    for copy in copies:
        copy.start()
    for i, flip in enumerate(FLIPS):
        x_ref[g ^ flip] = ins[i][...]

    def step(kb, carry):
        rows = pl.ds(pl.multiple_of(kb * 16, 16), 16)
        for sf in range(2):
            for a in range(4):
                values = [(x_ref[s, 0, sf, a, rows, :], x_ref[s, 1, sf, a, rows, :]) for s in range(8)]
                for m1, value in enumerate(fourier(values, -1)):
                    re, im = times(*value, unit(-1, a * m1, 32))
                    m_ref[m1, a, 0], m_ref[m1, a, 1] = re, im
            for m1 in range(8):
                values = fourier([(m_ref[m1, a, 0], m_ref[m1, a, 1]) for a in range(4)], -1)
                for m2, (re, im) in enumerate(values):
                    m = m1 + 8 * m2
                    tr, ti = twist_ref[2 * m : 2 * m + 1, :], twist_ref[2 * m + 1 : 2 * m + 2, :]
                    d_ref[pl.ds(512 * sf + 16 * m, 16), :128] = re * tr - im * ti
                    d_ref[pl.ds(512 * sf + 16 * m, 16), 128:] = re * ti + im * tr
        high, low = split(d_ref[...])
        d = three(high, low, lane_ref[:, :256], lane_ref[:, 256:])
        sr, si, fr, fi = d[:512, :128], d[:512, 128:], d[512:, :128], d[512:, 128:]
        high, low = split(jnp.concatenate([sr * fr - si * fi, sr * fi + si * fr], axis=1))
        d_ref[pl.ds(0, 512), :] = three(high, low, lane_ref[:, :256], lane_ref[:, 256:], 1)
        for m1 in range(8):
            values = []
            for m2 in range(4):
                m = m1 + 8 * m2
                tr, ti = twist_ref[2 * m : 2 * m + 1, :], twist_ref[2 * m + 1 : 2 * m + 2, :]
                re, im = d_ref[pl.ds(16 * m, 16), :128], d_ref[pl.ds(16 * m, 16), 128:]
                values.append((re * tr + im * ti, im * tr - re * ti))
            for a, value in enumerate(fourier(values, 1)):
                re, im = times(*value, unit(1, a * m1, 32))
                m_ref[m1, a, 0], m_ref[m1, a, 1] = re, im
        for a in range(4):
            values = fourier([(m_ref[m1, a, 0], m_ref[m1, a, 1]) for m1 in range(8)], 1)
            for at, (re, im) in enumerate(values):
                y_ref[at, 0, a, rows, :], y_ref[at, 1, a, rows, :] = re, im
        return carry

    lax.fori_loop(0, 2, step, 0)
    for i, flip in enumerate(BACK_FLIPS):
        outs[i][...] = y_ref[o ^ flip]
    for copy in copies:
        copy.wait()


def middle(place, blocks, lane, twist, turn):
    block = (2, 4, 32, LANES)
    return pl.pallas_call(
        middle_kernel,
        out_shape=[jax.ShapeDtypeStruct(block, jnp.float32)] * 8
        + [jax.ShapeDtypeStruct((2, 256, 512), jnp.float32)],
        in_specs=[SMEM] + [VMEM] * 10 + [HBM],
        out_specs=[VMEM] * 9,
        scratch_shapes=[
            pltpu.VMEM((8, 2, 2, 4, 32, LANES), jnp.float32),
            pltpu.VMEM((8, 4, 2, 16, LANES), jnp.float32),
            pltpu.VMEM((1024, 256), jnp.float32),
            pltpu.VMEM((8, 2, 4, 32, LANES), jnp.float32),
            pltpu.SemaphoreType.DMA((4,)),
        ],
        compiler_params=PARAMS,
    )(place, *blocks, lane, twist, turn)


def back_kernel(place_ref, *refs):
    ins, (back_ref, turn_ref), out_ref, (y2_ref,) = refs[:8], refs[8:10], refs[10], refs[11:]
    g = place_ref[2]
    for i, flip in enumerate(BACK_FLIPS):
        at = pl.multiple_of((g ^ flip) * 32, 32)
        for a in range(4):
            cols = pl.ds(128 * a, 128)
            tr, ti = turn_ref[0, pl.ds(at, 32), cols], turn_ref[1, pl.ds(at, 32), cols]
            re, im = ins[i][0, a], ins[i][1, a]
            for part, value in enumerate((re * tr + im * ti, im * tr - re * ti)):
                high, low = split(value)
                y2_ref[pl.ds(256 * part + at, 32), cols] = high
                y2_ref[pl.ds(512 + 256 * part + at, 32), cols] = low
    for n in range(2):
        cols = pl.ds(256 * n, 256)
        y = three(back_ref[:, :512], back_ref[:, 512:], y2_ref[:512, cols], y2_ref[512:, cols])
        for a in range(2):
            out_ref[pl.ds(2 * n + a, 256, stride=4), :] = y[:, 128 * a : 128 * (a + 1)]


def back(place, blocks, table, turn):
    return pl.pallas_call(
        back_kernel,
        out_shape=jax.ShapeDtypeStruct((1024, LANES), jnp.float32),
        in_specs=[SMEM] + [VMEM] * 10,
        out_specs=VMEM,
        scratch_shapes=[pltpu.VMEM((1024, 512), jnp.bfloat16)],
        compiler_params=PARAMS,
    )(place, *blocks, table, turn)


def unpack_kernel(place_ref, x_ref, out_ref, rows_ref, block_ref, sems):
    odd = place_ref[4]
    for o in range(4):
        for row in range(8):
            y, z = 2 * (row >> 2) + (o >> 1), 2 * (row & 3) + (o & 1)
            start = pl.multiple_of((((y + odd) & 3) * 8 + ((z + odd) & 7)) * 32, 32)
            rows_ref[pl.ds((o * 8 + row) * 32, 32), :] = x_ref[pl.ds(start, 32), :]
    copies = []
    for jl in range(4):
        for o in range(8):
            for a in range(4):
                start = (o >> 1) * 256 + (o & 1) * 16 + jl * 4 + a
                block_ref[jl, :, pl.ds(128 * (4 * o + a), 128)] = rows_ref[pl.ds(start, 8, stride=32), :]
        copies.append(pltpu.make_async_copy(block_ref.at[jl], out_ref.at[:, pl.ds(4096 * jl, 4096)], sems.at[jl]))
        copies[-1].start()
    for copy in copies:
        copy.wait()


def unpack(place, x):
    return pl.pallas_call(
        unpack_kernel,
        out_shape=jax.ShapeDtypeStruct((8, 16384), jnp.float32),
        in_specs=[SMEM, VMEM],
        out_specs=HBM,
        scratch_shapes=[
            pltpu.VMEM((1024, LANES), jnp.float32),
            pltpu.VMEM((4, 8, 4096), jnp.float32),
            pltpu.SemaphoreType.DMA((4,)),
        ],
        compiler_params=PARAMS,
    )(place, x)


def exchange(parts, pairs, flips):
    moved = [lax.ppermute(part, AXES, pairs(flip)) for part, flip in zip(parts, flips)]
    return moved + list(parts[len(flips) :])


def body(signal, filter_taps, skip_gain):
    known = tables()
    seq, x = lax.axis_index("seq"), lax.axis_index("tp")
    y, z, core = seq // 16, (seq // 2) % 8, seq % 2
    dy, dz, dx = (y - core) % 2, (z - core) % 2, (x - core) % 2
    g = 4 * dy + 2 * dz + dx
    row = ((y - core) % 4) // 2 * 4 + ((z - core) % 8) // 2
    first = 4 * dy + 2 * dz + (dx ^ core)
    odd = x % 2
    o = 4 * ((y - odd) % 2) + 2 * ((z - odd) % 2) + core
    place = jnp.stack([g, first, o ^ odd, o, odd]).astype(jnp.int32)
    gain = jnp.where(g == 0, skip_gain[row], 0.0).reshape(1)

    packed = pack(signal, filter_taps).reshape(256, 8, LANES)
    tokens = lax.all_to_all(packed, AXES, split_axis=0, concat_axis=0, tiled=True)
    names = ("turn", "ahead", "lane", "twist", "back")
    turn, table, lane, twist, untable = (jnp.asarray(known[name]) for name in names)
    table = lax.dynamic_index_in_dim(table, core, keepdims=False)
    turn_in = lax.dynamic_index_in_dim(turn, g, keepdims=False)
    parts = ahead(place, gain, tokens.reshape(2048, LANES), table, turn_in)
    parts = exchange(parts, among_members, FLIPS[:7])
    *parts, turn = middle(place, parts, lane, twist, turn)
    parts = exchange(parts, to_keepers, BACK_FLIPS)
    result = back(place, parts, untable, turn)
    result = lax.all_to_all(result.reshape(64, 16, LANES), "seq", split_axis=0, concat_axis=0, tiled=True)
    return unpack(place, result.reshape(1024, LANES))


def solution(mesh):
    placed = (P(None, ("seq", "tp")), P(None, ("seq", "tp")), P("tp"))
    return jax.shard_map(
        body, mesh=mesh, in_specs=placed, out_specs=P("tp", "seq"), check_vma=False
    )
```

```python
import functools
import math

import jax
import jax.numpy as jnp
import ml_dtypes
import numpy as np
from jax import lax
from jax.experimental import pallas as pl
from jax.experimental.pallas import tpu as pltpu
from jax.sharding import PartitionSpec as P

LENGTH = 1 << 20
BLOCKS = 256
LANES = 128
AXES = ("seq", "tp")
FLIPS = (7, 6, 5, 3, 4, 2, 1, 0)
BACK_FLIPS = (6, 7, 2, 3, 4, 5, 0, 1)
VMEM = pl.BlockSpec(memory_space=pltpu.VMEM)
HBM = pl.BlockSpec(memory_space=pltpu.HBM)
SMEM = pl.BlockSpec(memory_space=pltpu.SMEM)
PARAMS = pltpu.CompilerParams(vmem_limit_bytes=48 * 1024 * 1024)


def device(y, z, core, x):
    return (((y % 4) * 8 + z % 8) * 2 + core) * 4 + x % 4


def member(slab, row, g):
    core = slab % 2
    y = 2 * (row // 4) + core + (g >> 2)
    z = 2 * (row % 4) + core + ((g >> 1) & 1)
    return device(y, z, core, slab + (g & 1))


def keeper(slab, row, o):
    odd = slab % 2
    return device(2 * (row // 4) + odd + (o >> 2), 2 * (row % 4) + odd + ((o >> 1) & 1), o & 1, slab)


GROUPS = [(slab, row) for slab in range(4) for row in range(8)]


def among_members(flip):
    return [(member(s, r, g), member(s, r, g ^ flip)) for s, r in GROUPS for g in range(8)]


def to_keepers(flip):
    return [(member(s, r, g), keeper(s, r, first_range(s % 2, g) ^ flip)) for s, r in GROUPS for g in range(8)]


def first_range(core, g):
    return (g & 6) | ((g & 1) ^ core)


def halves(x):
    high = x.astype(ml_dtypes.bfloat16)
    low = (x - high.astype(np.float64)).astype(ml_dtypes.bfloat16)
    return high, low


@functools.cache
def tables():
    j = np.arange(BLOCKS)[:, None]
    k = np.arange(BLOCKS)[None, :] + 0.25
    angle = 2.0 * math.pi * ((j * k) % BLOCKS) / BLOCKS
    cos, sin = np.cos(angle), np.sin(angle)
    ahead_high, ahead_low = halves(np.concatenate([cos.T, -sin.T], axis=0))
    back_high, back_low = halves(np.concatenate([cos, -sin], axis=1) / LENGTH)
    t = np.arange(4096)[:, None]
    angle = (2.0 * math.pi / LENGTH) * (t * k)
    turn = np.stack([np.cos(angle), -np.sin(angle)])
    turn = turn.reshape(2, 8, 512, BLOCKS).transpose(1, 0, 3, 2).astype(np.float32)
    b = np.arange(LANES)
    angle = 2.0 * math.pi * ((b[:, None] * b[None, :]) % LANES) / LANES
    cos, sin = np.cos(angle), np.sin(angle)
    lane_high, lane_low = halves(np.block([[cos, -sin], [sin, cos]]))
    angle = (2.0 * math.pi / 4096) * (np.arange(32)[:, None] * b[None, :])
    twist = np.stack([np.cos(angle), -np.sin(angle)], axis=1)
    return dict(
        ahead=np.stack([np.concatenate([ahead_high, ahead_low], axis=1)] * 2),
        back=np.concatenate([back_high, back_low], axis=1),
        turn=turn,
        lane=np.concatenate([lane_high, lane_low], axis=1),
        twist=twist.astype(np.float32).reshape(64, LANES),
    )


def split(x):
    high = x.astype(jnp.bfloat16)
    return high, (x - high.astype(jnp.float32)).astype(jnp.bfloat16)


def dot(a, b, side=0):
    return lax.dot_general(a, b, (((1,), (side,)), ((), ())), preferred_element_type=jnp.float32)


def three(a_high, a_low, b_high, b_low, side=0):
    return dot(a_high, b_high, side) + (dot(a_high, b_low, side) + dot(a_low, b_high, side))


def times(re, im, factor):
    c, s = factor.real, factor.imag
    if abs(s) < 1e-12:
        return (re, im) if c > 0 else (-re, -im)
    if abs(c) < 1e-12:
        return (-im, re) if s > 0 else (im, -re)
    if abs(abs(c) - abs(s)) < 1e-12:
        p, q = np.sign(c), np.sign(s)
        first = re - im if p == q else re + im
        second = im + re if p == q else im - re
        return first * np.float32(c), second * np.float32(c)
    c, s = np.float32(c), np.float32(s)
    return re * c - im * s, re * s + im * c


def fourier(values, sign):
    size = len(values)
    if size == 1:
        return values
    even, odd = fourier(values[0::2], sign), fourier(values[1::2], sign)
    first, second = [], []
    for i in range(size // 2):
        angle = sign * 2.0 * math.pi * i / size
        re, im = times(*odd[i], complex(math.cos(angle), math.sin(angle)))
        first.append((even[i][0] + re, even[i][1] + im))
        second.append((even[i][0] - re, even[i][1] - im))
    return first + second


def unit(sign, numerator, denominator):
    angle = sign * 2.0 * math.pi * numerator / denominator
    return complex(math.cos(angle), math.sin(angle))


def pack_kernel(signal_ref, taps_ref, out_ref, rows_ref, packed_ref, sems):
    def load(at, ref, slab):
        rows = pl.ds(256 * slab, 256)
        return pltpu.make_async_copy(ref.at[rows, :], rows_ref.at[at, rows, :], sems.at[at, slab])

    copies = [[load(at, ref, slab) for slab in range(4)] for at, ref in enumerate((signal_ref, taps_ref))]
    order = (0, 2, 1, 3)
    for slab in order:
        for at in range(2):
            copies[at][slab].start()
    stores = []
    for slab in order:
        for at in range(2):
            copies[at][slab].wait()
        core = slab % 2
        for row in range(8):
            for g in range(8):
                to = member(slab, row, g)
                for at in range(2):
                    start = (slab * 32 + 4 * g) * 8 + row
                    rows = rows_ref[at, pl.ds(start, 4, stride=8), :]
                    packed_ref[core, to // 8, to % 4, pl.ds(4 * at, 4), :] = rows
        if slab >= 2:
            for n in range(2):
                part = pl.ds(16 * n, 16)
                source, to = packed_ref.at[core, part], out_ref.at[part, core]
                stores.append(pltpu.make_async_copy(source, to, sems.at[2 + core, n]))
                stores[-1].start()
    for copy in stores:
        copy.wait()


def tiles(x):
    return x.reshape(4, 8, 32, LANES).swapaxes(1, 2).reshape(1024, LANES)


def pack(signal, taps):
    return pl.pallas_call(
        pack_kernel,
        out_shape=jax.ShapeDtypeStruct((32, 2, 4, 8, LANES), jnp.float32),
        in_specs=[HBM, HBM],
        out_specs=HBM,
        scratch_shapes=[
            pltpu.VMEM((2, 1024, LANES), jnp.float32),
            pltpu.VMEM((2, 32, 4, 8, LANES), jnp.float32),
            pltpu.SemaphoreType.DMA((4, 4)),
        ],
        compiler_params=pltpu.CompilerParams(vmem_limit_bytes=60 * 1024 * 1024),
    )(tiles(signal), tiles(taps))


def turn_copies(turn_ref, at, to_ref, sems):
    parts = [(i, pl.ds(128 * h, 128)) for i in range(2) for h in range(2)]
    return [
        pltpu.make_async_copy(turn_ref.at[at, i, rows], to_ref.at[i, rows], sems.at[n])
        for n, (i, rows) in enumerate(parts)
    ]


def ahead_kernel(place_ref, gain_ref, x_ref, ahead_ref, turn_ref, *rest):
    outs, (x2_ref, y_ref) = rest[:8], rest[8:]
    g = place_ref[0]
    for s in range(8):
        x = x_ref[pl.ds(s, 256, stride=8), :]
        if s == 4:
            row = lax.broadcasted_iota(jnp.int32, x.shape, 0)
            lane = lax.broadcasted_iota(jnp.int32, x.shape, 1)
            x = x + jnp.where((row == 0) & (lane == 0), gain_ref[0], 0.0)
        high, low = split(x)
        x2_ref[pl.ds(0, 256), pl.ds(128 * s, 128)] = high
        x2_ref[pl.ds(256, 256), pl.ds(128 * s, 128)] = low
    for n in range(4):
        cols = pl.ds(256 * n, 256)
        y_ref[:, cols] = three(ahead_ref[:, :256], ahead_ref[:, 256:], x2_ref[:256, cols], x2_ref[256:, cols])
    for i, flip in enumerate(FLIPS):
        to = pl.multiple_of((g ^ flip) * 32, 32)
        for a in range(4):
            tr = turn_ref[0, pl.ds(to, 32), pl.ds(128 * a, 128)]
            ti = turn_ref[1, pl.ds(to, 32), pl.ds(128 * a, 128)]
            for sf in range(2):
                cols = pl.ds(512 * sf + 128 * a, 128)
                re, im = y_ref[pl.ds(to, 32), cols], y_ref[pl.ds(256 + to, 32), cols]
                outs[i][0, sf, a] = re * tr - im * ti
                outs[i][1, sf, a] = re * ti + im * tr


def ahead(place, gain, x, table, turn):
    block = (2, 2, 4, 32, LANES)
    return pl.pallas_call(
        ahead_kernel,
        out_shape=[jax.ShapeDtypeStruct(block, jnp.float32)] * 8,
        in_specs=[SMEM, SMEM] + [VMEM] * 3,
        out_specs=[VMEM] * 8,
        scratch_shapes=[pltpu.VMEM((512, 1024), jnp.bfloat16), pltpu.VMEM((512, 1024), jnp.float32)],
        compiler_params=PARAMS,
    )(place, gain, x, table, turn)


def middle_kernel(place_ref, *refs):
    ins, (lane_ref, twist_ref, turn_ref) = refs[:8], refs[8:11]
    outs, angle_ref, (x_ref, m_ref, d_ref, y_ref, sems) = refs[11:19], refs[19], refs[20:]
    g, o = place_ref[0], place_ref[1]
    copies = turn_copies(turn_ref, place_ref[3], angle_ref, sems)
    for copy in copies:
        copy.start()
    for i, flip in enumerate(FLIPS):
        x_ref[g ^ flip] = ins[i][...]

    def step(kb, carry):
        rows = pl.ds(pl.multiple_of(kb * 16, 16), 16)
        for sf in range(2):
            for a in range(4):
                values = [(x_ref[s, 0, sf, a, rows, :], x_ref[s, 1, sf, a, rows, :]) for s in range(8)]
                for m1, value in enumerate(fourier(values, -1)):
                    re, im = times(*value, unit(-1, a * m1, 32))
                    m_ref[m1, a, 0], m_ref[m1, a, 1] = re, im
            for m1 in range(8):
                values = fourier([(m_ref[m1, a, 0], m_ref[m1, a, 1]) for a in range(4)], -1)
                for m2, (re, im) in enumerate(values):
                    m = m1 + 8 * m2
                    tr, ti = twist_ref[2 * m : 2 * m + 1, :], twist_ref[2 * m + 1 : 2 * m + 2, :]
                    d_ref[pl.ds(512 * sf + 16 * m, 16), :128] = re * tr - im * ti
                    d_ref[pl.ds(512 * sf + 16 * m, 16), 128:] = re * ti + im * tr
        high, low = split(d_ref[...])
        d = three(high, low, lane_ref[:, :256], lane_ref[:, 256:])
        sr, si, fr, fi = d[:512, :128], d[:512, 128:], d[512:, :128], d[512:, 128:]
        high, low = split(jnp.concatenate([sr * fr - si * fi, sr * fi + si * fr], axis=1))
        d_ref[pl.ds(0, 512), :] = three(high, low, lane_ref[:, :256], lane_ref[:, 256:], 1)
        for m1 in range(8):
            values = []
            for m2 in range(4):
                m = m1 + 8 * m2
                tr, ti = twist_ref[2 * m : 2 * m + 1, :], twist_ref[2 * m + 1 : 2 * m + 2, :]
                re, im = d_ref[pl.ds(16 * m, 16), :128], d_ref[pl.ds(16 * m, 16), 128:]
                values.append((re * tr + im * ti, im * tr - re * ti))
            for a, value in enumerate(fourier(values, 1)):
                re, im = times(*value, unit(1, a * m1, 32))
                m_ref[m1, a, 0], m_ref[m1, a, 1] = re, im
        for a in range(4):
            values = fourier([(m_ref[m1, a, 0], m_ref[m1, a, 1]) for m1 in range(8)], 1)
            for at, (re, im) in enumerate(values):
                y_ref[at, 0, a, rows, :], y_ref[at, 1, a, rows, :] = re, im
        return carry

    lax.fori_loop(0, 2, step, 0)
    for i, flip in enumerate(BACK_FLIPS):
        outs[i][...] = y_ref[o ^ flip]
    for copy in copies:
        copy.wait()


def middle(place, blocks, lane, twist, turn):
    block = (2, 4, 32, LANES)
    return pl.pallas_call(
        middle_kernel,
        out_shape=[jax.ShapeDtypeStruct(block, jnp.float32)] * 8
        + [jax.ShapeDtypeStruct((2, 256, 512), jnp.float32)],
        in_specs=[SMEM] + [VMEM] * 10 + [HBM],
        out_specs=[VMEM] * 9,
        scratch_shapes=[
            pltpu.VMEM((8, 2, 2, 4, 32, LANES), jnp.float32),
            pltpu.VMEM((8, 4, 2, 16, LANES), jnp.float32),
            pltpu.VMEM((1024, 256), jnp.float32),
            pltpu.VMEM((8, 2, 4, 32, LANES), jnp.float32),
            pltpu.SemaphoreType.DMA((4,)),
        ],
        compiler_params=PARAMS,
    )(place, *blocks, lane, twist, turn)


def back_kernel(place_ref, *refs):
    ins, (back_ref, turn_ref), out_ref, (y2_ref,) = refs[:8], refs[8:10], refs[10], refs[11:]
    g = place_ref[2]
    for i, flip in enumerate(BACK_FLIPS):
        at = pl.multiple_of((g ^ flip) * 32, 32)
        for a in range(4):
            cols = pl.ds(128 * a, 128)
            tr, ti = turn_ref[0, pl.ds(at, 32), cols], turn_ref[1, pl.ds(at, 32), cols]
            re, im = ins[i][0, a], ins[i][1, a]
            for part, value in enumerate((re * tr + im * ti, im * tr - re * ti)):
                high, low = split(value)
                y2_ref[pl.ds(256 * part + at, 32), cols] = high
                y2_ref[pl.ds(512 + 256 * part + at, 32), cols] = low
    for n in range(2):
        cols = pl.ds(256 * n, 256)
        y = three(back_ref[:, :512], back_ref[:, 512:], y2_ref[:512, cols], y2_ref[512:, cols])
        for a in range(2):
            out_ref[pl.ds(2 * n + a, 256, stride=4), :] = y[:, 128 * a : 128 * (a + 1)]


def back(place, blocks, table, turn):
    return pl.pallas_call(
        back_kernel,
        out_shape=jax.ShapeDtypeStruct((1024, LANES), jnp.float32),
        in_specs=[SMEM] + [VMEM] * 10,
        out_specs=VMEM,
        scratch_shapes=[pltpu.VMEM((1024, 512), jnp.bfloat16)],
        compiler_params=PARAMS,
    )(place, *blocks, table, turn)


def unpack_kernel(place_ref, x_ref, out_ref, rows_ref, block_ref, sems):
    odd = place_ref[4]
    for o in range(4):
        for row in range(8):
            y, z = 2 * (row >> 2) + (o >> 1), 2 * (row & 3) + (o & 1)
            start = pl.multiple_of((((y + odd) & 3) * 8 + ((z + odd) & 7)) * 32, 32)
            rows_ref[pl.ds((o * 8 + row) * 32, 32), :] = x_ref[pl.ds(start, 32), :]
    copies = []
    for jl in range(4):
        for o in range(8):
            for a in range(4):
                start = (o >> 1) * 256 + (o & 1) * 16 + jl * 4 + a
                block_ref[jl, :, pl.ds(128 * (4 * o + a), 128)] = rows_ref[pl.ds(start, 8, stride=32), :]
        copies.append(pltpu.make_async_copy(block_ref.at[jl], out_ref.at[:, pl.ds(4096 * jl, 4096)], sems.at[jl]))
        copies[-1].start()
    for copy in copies:
        copy.wait()


def unpack(place, x):
    return pl.pallas_call(
        unpack_kernel,
        out_shape=jax.ShapeDtypeStruct((8, 16384), jnp.float32),
        in_specs=[SMEM, VMEM],
        out_specs=HBM,
        scratch_shapes=[
            pltpu.VMEM((1024, LANES), jnp.float32),
            pltpu.VMEM((4, 8, 4096), jnp.float32),
            pltpu.SemaphoreType.DMA((4,)),
        ],
        compiler_params=PARAMS,
    )(place, x)


def exchange(parts, pairs, flips):
    moved = [lax.ppermute(part, AXES, pairs(flip)) for part, flip in zip(parts, flips)]
    return moved + list(parts[len(flips) :])


def body(signal, filter_taps, skip_gain):
    known = tables()
    seq, x = lax.axis_index("seq"), lax.axis_index("tp")
    y, z, core = seq // 16, (seq // 2) % 8, seq % 2
    dy, dz, dx = (y - core) % 2, (z - core) % 2, (x - core) % 2
    g = 4 * dy + 2 * dz + dx
    row = ((y - core) % 4) // 2 * 4 + ((z - core) % 8) // 2
    first = 4 * dy + 2 * dz + (dx ^ core)
    odd = x % 2
    o = 4 * ((y - odd) % 2) + 2 * ((z - odd) % 2) + core
    place = jnp.stack([g, first, o ^ odd, o, odd]).astype(jnp.int32)
    gain = jnp.where(g == 0, skip_gain[row], 0.0).reshape(1)

    packed = pack(signal, filter_taps).reshape(256, 8, LANES)
    tokens = lax.all_to_all(packed, AXES, split_axis=0, concat_axis=0, tiled=True)
    names = ("turn", "ahead", "lane", "twist", "back")
    turn, table, lane, twist, untable = (jnp.asarray(known[name]) for name in names)
    table = lax.dynamic_index_in_dim(table, core, keepdims=False)
    turn_in = lax.dynamic_index_in_dim(turn, g, keepdims=False)
    parts = ahead(place, gain, tokens.reshape(2048, LANES), table, turn_in)
    parts = exchange(parts, among_members, FLIPS[:7])
    *parts, turn = middle(place, parts, lane, twist, turn)
    parts = exchange(parts, to_keepers, BACK_FLIPS)
    result = back(place, parts, untable, turn)
    result = lax.all_to_all(result.reshape(64, 16, LANES), "seq", split_axis=0, concat_axis=0, tiled=True)
    return unpack(place, result.reshape(1024, LANES))


def solution(mesh):
    placed = (P(None, ("seq", "tp")), P(None, ("seq", "tp")), P("tp"))
    return jax.shard_map(
        body, mesh=mesh, in_specs=placed, out_specs=P("tp", "seq"), check_vma=False
    )
```

```python
import functools
import math

import jax
import jax.numpy as jnp
import ml_dtypes
import numpy as np
from jax import lax
from jax.experimental import pallas as pl
from jax.experimental.pallas import tpu as pltpu
from jax.sharding import PartitionSpec as P

LENGTH = 1 << 20
BLOCKS = 256
LANES = 128
AXES = ("seq", "tp")
FLIPS = (7, 6, 5, 3, 4, 2, 1, 0)
BACK_FLIPS = (7, 6, 5, 4, 3, 2, 1, 0)
VMEM = pl.BlockSpec(memory_space=pltpu.VMEM)
HBM = pl.BlockSpec(memory_space=pltpu.HBM)
SMEM = pl.BlockSpec(memory_space=pltpu.SMEM)
PARAMS = pltpu.CompilerParams(vmem_limit_bytes=48 * 1024 * 1024)


def device(y, z, core, x):
    return (((y % 4) * 8 + z % 8) * 2 + core) * 4 + x % 4


def member(slab, row, g):
    core = slab % 2
    y = 2 * (row // 4) + core + (g >> 2)
    z = 2 * (row % 4) + core + ((g >> 1) & 1)
    return device(y, z, core, slab + (g & 1))


def keeper(slab, row, o):
    odd = slab % 2
    return device(2 * (row // 4) + odd + (o >> 2), 2 * (row % 4) + odd + ((o >> 1) & 1), o & 1, slab)


GROUPS = [(slab, row) for slab in range(4) for row in range(8)]


def among_members(flip):
    return [(member(s, r, g), member(s, r, g ^ flip)) for s, r in GROUPS for g in range(8)]


def to_keepers(flip):
    return [(member(s, r, g), keeper(s, r, first_range(s % 2, g) ^ flip)) for s, r in GROUPS for g in range(8)]


def first_range(core, g):
    return (g & 6) | ((g & 1) ^ core)


def halves(x):
    high = x.astype(ml_dtypes.bfloat16)
    low = (x - high.astype(np.float64)).astype(ml_dtypes.bfloat16)
    return high, low


@functools.cache
def tables():
    j = np.arange(BLOCKS)[:, None]
    k = np.arange(BLOCKS)[None, :] + 0.25
    angle = 2.0 * math.pi * ((j * k) % BLOCKS) / BLOCKS
    cos, sin = np.cos(angle), np.sin(angle)
    ahead_high, ahead_low = halves(np.concatenate([cos.T, -sin.T], axis=0))
    back_high, back_low = halves(np.concatenate([cos, -sin], axis=1) / LENGTH)
    t = np.arange(4096)[:, None]
    angle = (2.0 * math.pi / LENGTH) * (t * k)
    turn = np.stack([np.cos(angle), -np.sin(angle)])
    turn = turn.reshape(2, 8, 512, BLOCKS).transpose(1, 0, 3, 2).astype(np.float32)
    b = np.arange(LANES)
    angle = 2.0 * math.pi * ((b[:, None] * b[None, :]) % LANES) / LANES
    cos, sin = np.cos(angle), np.sin(angle)
    lane_high, lane_low = halves(np.block([[cos, -sin], [sin, cos]]))
    angle = (2.0 * math.pi / 4096) * (np.arange(32)[:, None] * b[None, :])
    twist = np.stack([np.cos(angle), -np.sin(angle)], axis=1)
    return dict(
        ahead=np.stack([np.concatenate([ahead_high, ahead_low], axis=1)] * 2),
        back=np.concatenate([back_high, back_low], axis=1),
        turn=turn,
        lane=np.concatenate([lane_high, lane_low], axis=1),
        twist=twist.astype(np.float32).reshape(64, LANES),
    )


def split(x):
    high = x.astype(jnp.bfloat16)
    return high, (x - high.astype(jnp.float32)).astype(jnp.bfloat16)


def dot(a, b, side=0):
    return lax.dot_general(a, b, (((1,), (side,)), ((), ())), preferred_element_type=jnp.float32)


def three(a_high, a_low, b_high, b_low, side=0):
    return dot(a_high, b_high, side) + (dot(a_high, b_low, side) + dot(a_low, b_high, side))


def times(re, im, factor):
    c, s = factor.real, factor.imag
    if abs(s) < 1e-12:
        return (re, im) if c > 0 else (-re, -im)
    if abs(c) < 1e-12:
        return (-im, re) if s > 0 else (im, -re)
    if abs(abs(c) - abs(s)) < 1e-12:
        p, q = np.sign(c), np.sign(s)
        first = re - im if p == q else re + im
        second = im + re if p == q else im - re
        return first * np.float32(c), second * np.float32(c)
    c, s = np.float32(c), np.float32(s)
    return re * c - im * s, re * s + im * c


def fourier(values, sign):
    size = len(values)
    if size == 1:
        return values
    even, odd = fourier(values[0::2], sign), fourier(values[1::2], sign)
    first, second = [], []
    for i in range(size // 2):
        angle = sign * 2.0 * math.pi * i / size
        re, im = times(*odd[i], complex(math.cos(angle), math.sin(angle)))
        first.append((even[i][0] + re, even[i][1] + im))
        second.append((even[i][0] - re, even[i][1] - im))
    return first + second


def unit(sign, numerator, denominator):
    angle = sign * 2.0 * math.pi * numerator / denominator
    return complex(math.cos(angle), math.sin(angle))


def pack_kernel(signal_ref, taps_ref, out_ref, rows_ref, packed_ref, sems):
    def load(at, ref, slab):
        rows = pl.ds(256 * slab, 256)
        return pltpu.make_async_copy(ref.at[rows, :], rows_ref.at[at, rows, :], sems.at[at, slab])

    copies = [[load(at, ref, slab) for slab in range(4)] for at, ref in enumerate((signal_ref, taps_ref))]
    order = (0, 2, 1, 3)
    for slab in order:
        for at in range(2):
            copies[at][slab].start()
    stores = []
    for slab in order:
        for at in range(2):
            copies[at][slab].wait()
        core = slab % 2
        for row in range(8):
            for g in range(8):
                to = member(slab, row, g)
                for at in range(2):
                    start = (slab * 32 + 4 * g) * 8 + row
                    rows = rows_ref[at, pl.ds(start, 4, stride=8), :]
                    packed_ref[core, to // 8, to % 4, pl.ds(4 * at, 4), :] = rows
        if slab >= 2:
            for n in range(2):
                part = pl.ds(16 * n, 16)
                source, to = packed_ref.at[core, part], out_ref.at[part, core]
                stores.append(pltpu.make_async_copy(source, to, sems.at[2 + core, n]))
                stores[-1].start()
    for copy in stores:
        copy.wait()


def tiles(x):
    return x.reshape(4, 8, 32, LANES).swapaxes(1, 2).reshape(1024, LANES)


def pack(signal, taps):
    return pl.pallas_call(
        pack_kernel,
        out_shape=jax.ShapeDtypeStruct((32, 2, 4, 8, LANES), jnp.float32),
        in_specs=[HBM, HBM],
        out_specs=HBM,
        scratch_shapes=[
            pltpu.VMEM((2, 1024, LANES), jnp.float32),
            pltpu.VMEM((2, 32, 4, 8, LANES), jnp.float32),
            pltpu.SemaphoreType.DMA((4, 4)),
        ],
        compiler_params=pltpu.CompilerParams(vmem_limit_bytes=60 * 1024 * 1024),
    )(tiles(signal), tiles(taps))


def turn_copies(turn_ref, at, to_ref, sems):
    parts = [(i, pl.ds(128 * h, 128)) for i in range(2) for h in range(2)]
    return [
        pltpu.make_async_copy(turn_ref.at[at, i, rows], to_ref.at[i, rows], sems.at[n])
        for n, (i, rows) in enumerate(parts)
    ]


def ahead_kernel(place_ref, gain_ref, x_ref, ahead_ref, turn_ref, *rest):
    outs, (x2_ref, y_ref) = rest[:8], rest[8:]
    g = place_ref[0]
    for s in range(8):
        x = x_ref[pl.ds(s, 256, stride=8), :]
        if s == 4:
            row = lax.broadcasted_iota(jnp.int32, x.shape, 0)
            lane = lax.broadcasted_iota(jnp.int32, x.shape, 1)
            x = x + jnp.where((row == 0) & (lane == 0), gain_ref[0], 0.0)
        high, low = split(x)
        x2_ref[pl.ds(0, 256), pl.ds(128 * s, 128)] = high
        x2_ref[pl.ds(256, 256), pl.ds(128 * s, 128)] = low
    for n in range(4):
        cols = pl.ds(256 * n, 256)
        y_ref[:, cols] = three(ahead_ref[:, :256], ahead_ref[:, 256:], x2_ref[:256, cols], x2_ref[256:, cols])
    for i, flip in enumerate(FLIPS):
        to = pl.multiple_of((g ^ flip) * 32, 32)
        for a in range(4):
            tr = turn_ref[0, pl.ds(to, 32), pl.ds(128 * a, 128)]
            ti = turn_ref[1, pl.ds(to, 32), pl.ds(128 * a, 128)]
            for sf in range(2):
                cols = pl.ds(512 * sf + 128 * a, 128)
                re, im = y_ref[pl.ds(to, 32), cols], y_ref[pl.ds(256 + to, 32), cols]
                outs[i][0, sf, a] = re * tr - im * ti
                outs[i][1, sf, a] = re * ti + im * tr


def ahead(place, gain, x, table, turn):
    block = (2, 2, 4, 32, LANES)
    return pl.pallas_call(
        ahead_kernel,
        out_shape=[jax.ShapeDtypeStruct(block, jnp.float32)] * 8,
        in_specs=[SMEM, SMEM] + [VMEM] * 3,
        out_specs=[VMEM] * 8,
        scratch_shapes=[pltpu.VMEM((512, 1024), jnp.bfloat16), pltpu.VMEM((512, 1024), jnp.float32)],
        compiler_params=PARAMS,
    )(place, gain, x, table, turn)


def middle_kernel(place_ref, *refs):
    ins, (lane_ref, twist_ref, turn_ref) = refs[:8], refs[8:11]
    outs, angle_ref, (x_ref, m_ref, d_ref, y_ref, sems) = refs[11:19], refs[19], refs[20:]
    g, o = place_ref[0], place_ref[1]
    copies = turn_copies(turn_ref, place_ref[3], angle_ref, sems)
    for copy in copies:
        copy.start()
    for i, flip in enumerate(FLIPS):
        x_ref[g ^ flip] = ins[i][...]

    def step(kb, carry):
        rows = pl.ds(pl.multiple_of(kb * 16, 16), 16)
        for sf in range(2):
            for a in range(4):
                values = [(x_ref[s, 0, sf, a, rows, :], x_ref[s, 1, sf, a, rows, :]) for s in range(8)]
                for m1, value in enumerate(fourier(values, -1)):
                    re, im = times(*value, unit(-1, a * m1, 32))
                    m_ref[m1, a, 0], m_ref[m1, a, 1] = re, im
            for m1 in range(8):
                values = fourier([(m_ref[m1, a, 0], m_ref[m1, a, 1]) for a in range(4)], -1)
                for m2, (re, im) in enumerate(values):
                    m = m1 + 8 * m2
                    tr, ti = twist_ref[2 * m : 2 * m + 1, :], twist_ref[2 * m + 1 : 2 * m + 2, :]
                    d_ref[pl.ds(512 * sf + 16 * m, 16), :128] = re * tr - im * ti
                    d_ref[pl.ds(512 * sf + 16 * m, 16), 128:] = re * ti + im * tr
        high, low = split(d_ref[...])
        d = three(high, low, lane_ref[:, :256], lane_ref[:, 256:])
        sr, si, fr, fi = d[:512, :128], d[:512, 128:], d[512:, :128], d[512:, 128:]
        high, low = split(jnp.concatenate([sr * fr - si * fi, sr * fi + si * fr], axis=1))
        d_ref[pl.ds(0, 512), :] = three(high, low, lane_ref[:, :256], lane_ref[:, 256:], 1)
        for m1 in range(8):
            values = []
            for m2 in range(4):
                m = m1 + 8 * m2
                tr, ti = twist_ref[2 * m : 2 * m + 1, :], twist_ref[2 * m + 1 : 2 * m + 2, :]
                re, im = d_ref[pl.ds(16 * m, 16), :128], d_ref[pl.ds(16 * m, 16), 128:]
                values.append((re * tr + im * ti, im * tr - re * ti))
            for a, value in enumerate(fourier(values, 1)):
                re, im = times(*value, unit(1, a * m1, 32))
                m_ref[m1, a, 0], m_ref[m1, a, 1] = re, im
        for a in range(4):
            values = fourier([(m_ref[m1, a, 0], m_ref[m1, a, 1]) for m1 in range(8)], 1)
            for at, (re, im) in enumerate(values):
                y_ref[at, 0, a, rows, :], y_ref[at, 1, a, rows, :] = re, im
        return carry

    lax.fori_loop(0, 2, step, 0)
    for i, flip in enumerate(BACK_FLIPS):
        outs[i][...] = y_ref[o ^ flip]
    for copy in copies:
        copy.wait()


def middle(place, blocks, lane, twist, turn):
    block = (2, 4, 32, LANES)
    return pl.pallas_call(
        middle_kernel,
        out_shape=[jax.ShapeDtypeStruct(block, jnp.float32)] * 8
        + [jax.ShapeDtypeStruct((2, 256, 512), jnp.float32)],
        in_specs=[SMEM] + [VMEM] * 10 + [HBM],
        out_specs=[VMEM] * 9,
        scratch_shapes=[
            pltpu.VMEM((8, 2, 2, 4, 32, LANES), jnp.float32),
            pltpu.VMEM((8, 4, 2, 16, LANES), jnp.float32),
            pltpu.VMEM((1024, 256), jnp.float32),
            pltpu.VMEM((8, 2, 4, 32, LANES), jnp.float32),
            pltpu.SemaphoreType.DMA((4,)),
        ],
        compiler_params=PARAMS,
    )(place, *blocks, lane, twist, turn)


def back_kernel(place_ref, *refs):
    ins, (back_ref, turn_ref), out_ref, (y2_ref,) = refs[:8], refs[8:10], refs[10], refs[11:]
    g = place_ref[2]
    for i, flip in enumerate(BACK_FLIPS):
        at = pl.multiple_of((g ^ flip) * 32, 32)
        for a in range(4):
            cols = pl.ds(128 * a, 128)
            tr, ti = turn_ref[0, pl.ds(at, 32), cols], turn_ref[1, pl.ds(at, 32), cols]
            re, im = ins[i][0, a], ins[i][1, a]
            for part, value in enumerate((re * tr + im * ti, im * tr - re * ti)):
                high, low = split(value)
                y2_ref[pl.ds(256 * part + at, 32), cols] = high
                y2_ref[pl.ds(512 + 256 * part + at, 32), cols] = low
    for n in range(2):
        cols = pl.ds(256 * n, 256)
        y = three(back_ref[:, :512], back_ref[:, 512:], y2_ref[:512, cols], y2_ref[512:, cols])
        for a in range(2):
            out_ref[pl.ds(2 * n + a, 256, stride=4), :] = y[:, 128 * a : 128 * (a + 1)]


def back(place, blocks, table, turn):
    return pl.pallas_call(
        back_kernel,
        out_shape=jax.ShapeDtypeStruct((1024, LANES), jnp.float32),
        in_specs=[SMEM] + [VMEM] * 10,
        out_specs=VMEM,
        scratch_shapes=[pltpu.VMEM((1024, 512), jnp.bfloat16)],
        compiler_params=PARAMS,
    )(place, *blocks, table, turn)


def unpack_kernel(place_ref, x_ref, out_ref, rows_ref, block_ref, sems):
    odd = place_ref[4]
    for o in range(4):
        for row in range(8):
            y, z = 2 * (row >> 2) + (o >> 1), 2 * (row & 3) + (o & 1)
            start = pl.multiple_of((((y + odd) & 3) * 8 + ((z + odd) & 7)) * 32, 32)
            rows_ref[pl.ds((o * 8 + row) * 32, 32), :] = x_ref[pl.ds(start, 32), :]
    copies = []
    for jl in range(4):
        for o in range(8):
            for a in range(4):
                start = (o >> 1) * 256 + (o & 1) * 16 + jl * 4 + a
                block_ref[jl, :, pl.ds(128 * (4 * o + a), 128)] = rows_ref[pl.ds(start, 8, stride=32), :]
        copies.append(pltpu.make_async_copy(block_ref.at[jl], out_ref.at[:, pl.ds(4096 * jl, 4096)], sems.at[jl]))
        copies[-1].start()
    for copy in copies:
        copy.wait()


def unpack(place, x):
    return pl.pallas_call(
        unpack_kernel,
        out_shape=jax.ShapeDtypeStruct((8, 16384), jnp.float32),
        in_specs=[SMEM, VMEM],
        out_specs=HBM,
        scratch_shapes=[
            pltpu.VMEM((1024, LANES), jnp.float32),
            pltpu.VMEM((4, 8, 4096), jnp.float32),
            pltpu.SemaphoreType.DMA((4,)),
        ],
        compiler_params=PARAMS,
    )(place, x)


def exchange(parts, pairs, flips):
    moved = [lax.ppermute(part, AXES, pairs(flip)) for part, flip in zip(parts, flips)]
    return moved + list(parts[len(flips) :])


def body(signal, filter_taps, skip_gain):
    known = tables()
    seq, x = lax.axis_index("seq"), lax.axis_index("tp")
    y, z, core = seq // 16, (seq // 2) % 8, seq % 2
    dy, dz, dx = (y - core) % 2, (z - core) % 2, (x - core) % 2
    g = 4 * dy + 2 * dz + dx
    row = ((y - core) % 4) // 2 * 4 + ((z - core) % 8) // 2
    first = 4 * dy + 2 * dz + (dx ^ core)
    odd = x % 2
    o = 4 * ((y - odd) % 2) + 2 * ((z - odd) % 2) + core
    place = jnp.stack([g, first, o ^ odd, o, odd]).astype(jnp.int32)
    gain = jnp.where(g == 0, skip_gain[row], 0.0).reshape(1)

    packed = pack(signal, filter_taps).reshape(256, 8, LANES)
    tokens = lax.all_to_all(packed, AXES, split_axis=0, concat_axis=0, tiled=True)
    names = ("turn", "ahead", "lane", "twist", "back")
    turn, table, lane, twist, untable = (jnp.asarray(known[name]) for name in names)
    table = lax.dynamic_index_in_dim(table, core, keepdims=False)
    turn_in = lax.dynamic_index_in_dim(turn, g, keepdims=False)
    parts = ahead(place, gain, tokens.reshape(2048, LANES), table, turn_in)
    parts = exchange(parts, among_members, FLIPS[:7])
    *parts, turn = middle(place, parts, lane, twist, turn)
    parts = exchange(parts, to_keepers, BACK_FLIPS)
    result = back(place, parts, untable, turn)
    result = lax.all_to_all(result.reshape(64, 16, LANES), "seq", split_axis=0, concat_axis=0, tiled=True)
    return unpack(place, result.reshape(1024, LANES))


def solution(mesh):
    placed = (P(None, ("seq", "tp")), P(None, ("seq", "tp")), P("tp"))
    return jax.shard_map(
        body, mesh=mesh, in_specs=placed, out_specs=P("tp", "seq"), check_vma=False
    )
```
